512 devices in a mesh: seq: 128 (over z, y, core), pair: 4 (over x).
Axes of the slice: x: 4, y: 8, z: 8, core: 2. Of those that a mesh axis runs over, the one named last changes fastest.
Arguments:
- query_rows: bfloat16 [65536, 2560], P(('seq', 'pair')), may hold values from -6 to 6
- key_rows: bfloat16 [65536, 2560], P(('seq', 'pair')), may hold values from -6 to 6
- value_rows: bfloat16 [65536, 2560], P(('seq', 'pair')), may hold values from -6 to 6
- grad_out: bfloat16 [65536, 2560], P(('seq', 'pair')), may hold values from -24 to 24
- log_sum_exp: float32 [20, 65536], P(None, ('seq', 'pair')), may hold values from 0 to 10, as said below
- row_delta: float32 [20, 65536], P(None, ('seq', 'pair')), may hold values from -18 to 18
- block_counts: int32 [512], P(('seq', 'pair')), may hold values from 1 to 4, as said below
Outputs:
- grad_query: bfloat16 [65536, 2560], P(('seq', 'pair'))
- grad_key: bfloat16 [65536, 2560], P(('seq', 'pair'))
- grad_value: bfloat16 [65536, 2560], P(('seq', 'pair'))
The draws below stay inside these ranges and needn't reach their ends.
Inputs may be any that keep to these rules, and one draw needn't show every extreme that they name: block_counts[0] is 1, and every later entry is either 1 (a document starts there) or one more than the entry before it; the first 4 entries and the last 4 entries are 1, 2, ... up to 4. `log_sum_exp`: each entry lies within one half of ln(m) + 0.5, m the number of positions that row is allowed to attend.
All inputs are finite; a program needn't handle non-finite values.
Results may differ from the reference program's by a relative error of at most 0.0056.
Values may be sent and summed in bfloat16 or wider, within the bound.
A program may use at most 64 MiB of HBM per device.

```python
import jax
import jax.numpy as jnp
from jax import lax

HEADS = 20
HEAD_DIM = 128
TOK_DEV = 128
REACH = 4
BLOCKS = 512
TOKENS = 65536
WIDTH = 2560


def document_counts(key):
    count_key = jax.random.fold_in(key, 11)
    lengths = jax.random.randint(count_key, (BLOCKS,), 1, REACH + 1, dtype=jnp.int32)
    lengths = lengths.at[0].set(REACH)
    starts = jnp.cumsum(lengths, dtype=jnp.int32) - lengths
    marks = jnp.zeros((BLOCKS,), jnp.int32).at[starts].set(1, mode='drop')
    places = jnp.arange(BLOCKS, dtype=jnp.int32)
    latest = lax.cummax(jnp.where(marks > 0, places, 0), axis=0)
    counts = places - latest + 1
    tail = jnp.arange(1, REACH + 1, dtype=jnp.int32)
    return counts.at[BLOCKS - REACH:].set(tail)


def draw_block_counts(key, part):
    return document_counts(key)


def draw_log_sum_exp(key, part):
    counts = document_counts(key)
    key = jax.random.fold_in(key, 5)
    places = jnp.arange(TOK_DEV, dtype=jnp.int32)
    attended = ((counts[:, None] - 1) * TOK_DEV + places[None, :] + 1).reshape(TOKENS).astype(jnp.float32)
    jitter_rows = jax.random.uniform(key, (HEADS, TOKENS), jnp.float32, -0.5, 0.5)
    return jnp.log(attended)[None, :] + 0.5 + jitter_rows


def block_scale(stream_key, shape, cuts, smallest, largest):
    def one(dim, blocks):
        heights = jax.random.uniform(jax.random.fold_in(jax.random.fold_in(stream_key, 6), dim), (blocks,), jnp.float32, smallest / len(cuts), largest / len(cuts))
        return jnp.repeat(jnp.exp(heights), shape[dim] // blocks).reshape((-1,) + (1,) * (len(shape) - dim - 1))

    level = one(*cuts[0])
    for cut in cuts[1:]:
        level = level * one(*cut)
    return level


def centred(key, shape, scale, most, shards=(), kind=jnp.bfloat16):
    values = jax.random.normal(key, shape, jnp.float32) * scale
    if len(shards) > 0:
        values = block_scale(key, shape, shards, -0.22, 0.18) * values
    return jnp.clip(values, min=-most, max=most).astype(kind)


def setup_inputs(seed: int = 0) -> dict:
    arg_keys = jax.random.split(jax.random.key(seed), 8)
    query_rows = centred(arg_keys[0], (TOKENS, WIDTH), 1.0, 6.0, ((0, 512),))
    key_rows = centred(arg_keys[1], (TOKENS, WIDTH), 1.0, 6.0, ((0, 512),))
    value_rows = centred(arg_keys[2], (TOKENS, WIDTH), 1.0, 6.0, ((0, 512),))
    grad_out = centred(arg_keys[3], (TOKENS, WIDTH), 4.0, 24.0, ((0, 512),))
    log_sum_exp = draw_log_sum_exp(jax.random.fold_in(arg_keys[7], 71), 0)
    row_delta = centred(arg_keys[5], (HEADS, TOKENS), 3.0, 18.0, ((1, 512),), jnp.float32)
    block_counts = draw_block_counts(jax.random.fold_in(arg_keys[7], 71), 0)
    return dict(query_rows=query_rows, key_rows=key_rows, value_rows=value_rows, grad_out=grad_out, log_sum_exp=log_sum_exp, row_delta=row_delta, block_counts=block_counts)


def tile_terms(query_blk, grad_blk, lse_blk, delta_blk, key_blk, value_blk, allowed):
    scaling = HEAD_DIM ** -0.5
    highest = lax.Precision.HIGHEST
    query_f = query_blk.astype(jnp.float32)
    grad_f = grad_blk.astype(jnp.float32)
    key_f = key_blk.astype(jnp.float32)
    value_f = value_blk.astype(jnp.float32)
    scores = jnp.einsum("qhe,khe->hqk", query_f, key_f, precision=highest) * scaling
    attention = jnp.where(allowed[None], jnp.exp(scores - lse_blk[:, :, None]), 0.0)
    attention_half = lax.optimization_barrier(attention.astype(jnp.bfloat16)).astype(jnp.float32)
    value_grad = jnp.einsum("hqk,qhe->khe", attention_half, grad_f, precision=highest)
    dprobs = jnp.einsum("qhe,khe->hqk", grad_f, value_f, precision=highest)
    dscores = (attention * (dprobs - delta_blk[:, :, None]) * scaling).astype(jnp.bfloat16)
    dscores_f = lax.optimization_barrier(dscores).astype(jnp.float32)
    query_grad = jnp.einsum("hqk,khe->qhe", dscores_f, key_f, precision=highest)
    key_grad = jnp.einsum("hqk,qhe->khe", dscores_f, query_f, precision=highest)
    return query_grad, key_grad, value_grad


def reference(query_rows, key_rows, value_rows, grad_out, log_sum_exp, row_delta, block_counts):
    block_shape = (BLOCKS, TOK_DEV, HEADS, HEAD_DIM)
    queries = query_rows.reshape(block_shape)
    key_blocks = key_rows.reshape(block_shape)
    values = value_rows.reshape(block_shape)
    grad_blocks = grad_out.reshape(block_shape)
    lse_blocks = log_sum_exp.reshape(HEADS, BLOCKS, TOK_DEV).transpose(1, 0, 2)
    delta_blocks = row_delta.reshape(HEADS, BLOCKS, TOK_DEV).transpose(1, 0, 2)
    inside = jnp.arange(TOK_DEV, dtype=jnp.int32)
    causal = inside[:, None] >= inside[None, :]
    zero_acc = jnp.zeros((REACH, TOK_DEV, HEADS, HEAD_DIM), jnp.float32)

    def visit(running, block_id):
        key_acc, value_acc = running
        new_slot = jnp.zeros((1, TOK_DEV, HEADS, HEAD_DIM), jnp.float32)
        key_acc = jnp.concatenate([key_acc[1:], new_slot], axis=0)
        value_acc = jnp.concatenate([value_acc[1:], new_slot], axis=0)
        query_sum = jnp.zeros((TOK_DEV, HEADS, HEAD_DIM), jnp.float32)
        for distance in range(REACH):
            source = (block_id - distance) % BLOCKS
            within = distance < block_counts[block_id]
            pattern = causal if distance == 0 else jnp.ones_like(causal)
            allowed = jnp.logical_and(within, pattern)
            query_part, key_part, value_part = tile_terms(
                queries[block_id], grad_blocks[block_id], lse_blocks[block_id], delta_blocks[block_id],
                key_blocks[source], values[source], allowed)
            query_sum = query_sum + query_part
            key_acc = key_acc.at[REACH - 1 - distance].add(key_part)
            value_acc = value_acc.at[REACH - 1 - distance].add(value_part)
        emitted = (key_acc[0].astype(jnp.bfloat16), value_acc[0].astype(jnp.bfloat16), query_sum.astype(jnp.bfloat16))
        return (key_acc, value_acc), emitted

    finals, emitted = lax.scan(visit, (zero_acc, zero_acc), jnp.arange(BLOCKS, dtype=jnp.int32))
    key_done, value_done, query_done = emitted
    grad_key = jnp.concatenate([key_done[REACH - 1:], finals[0][1:].astype(jnp.bfloat16)], axis=0)
    grad_value = jnp.concatenate([value_done[REACH - 1:], finals[1][1:].astype(jnp.bfloat16)], axis=0)
    flat = (TOKENS, HEADS * HEAD_DIM)
    return (query_done.reshape(flat), grad_key.reshape(flat), grad_value.reshape(flat))
```

```python
import functools
import math

import jax
import jax.numpy as jnp
from jax import lax
from jax.experimental import pallas as pl
from jax.experimental.pallas import tpu as pltpu
from jax.sharding import PartitionSpec as P

MESH = pl.DeviceIdType.MESH
BLK = 128
DIM = 128
RING = 4
HALO = 3
LOG2E = math.log2(math.e)
NEVER = 1e30
NT = (((1,), (1,)), ((), ()))
TN = (((0,), (0,)), ((), ()))


def dot(a, b, dims=(((1,), (0,)), ((), ()))):
    return lax.dot_general(a, b, dims, preferred_element_type=jnp.float32)


def kernel(
    groups,
    per,
    q_hbm,
    k_hbm,
    v_hbm,
    g_hbm,
    lse_ref,
    delta_ref,
    cnt_ref,
    dq_hbm,
    dk_hbm,
    dv_hbm,
    in_buf,
    own_stats,
    stats,
    out_buf,
    ds_buf,
    in_send,
    in_recv,
    in_local_sem,
    halo_send,
    halo_recv,
    stat_send,
    stat_recv,
    stat_halo_send,
    stat_halo_recv,
    out_send,
    out_recv,
    out_local_sem,
):
    s = lax.axis_index("seq")
    x = lax.axis_index("pair")
    after = lax.rem(s + 1, groups)
    before = lax.rem(s + groups - 1, groups)
    scale = DIM ** (-0.5)

    own_stats[...] = jnp.zeros_like(own_stats)
    for c in range(RING):
        own_stats[c, 0:per] = lse_ref[c * per : (c + 1) * per, :] * LOG2E
        own_stats[c, per : 2 * per] = delta_ref[c * per : (c + 1) * per, :]
        own_stats[c, 2 * per : 2 * per + 1] = jnp.full((1, BLK), cnt_ref[0], jnp.int32).astype(
            jnp.float32
        )

    barrier = pltpu.get_barrier_semaphore()
    for d in range(1, RING):
        pl.semaphore_signal(
            barrier, 1, device_id=(s, lax.rem(x + d, RING)), device_id_type=MESH
        )
    pl.semaphore_signal(barrier, 1, device_id=(after, x), device_id_type=MESH)
    pl.semaphore_signal(barrier, 1, device_id=(before, x), device_id_type=MESH)
    pl.semaphore_wait(barrier, RING + 1)

    def cols(owner, j):
        return pl.ds(pl.multiple_of((owner * per + j) * DIM, DIM), DIM)

    sources = (k_hbm, v_hbm, q_hbm, g_hbm)
    first = (HALO, HALO, 0, 0)
    outs = (dq_hbm, dk_hbm, dv_hbm)

    def copy_to(src, dst, send, recv, device):
        return pltpu.make_async_remote_copy(
            src_ref=src,
            dst_ref=dst,
            send_sem=send,
            recv_sem=recv,
            device_id=device,
            device_id_type=MESH,
        )

    def covers(ref, send, recv):
        return copy_to(ref, ref, send, recv, (after, x))

    def in_copy(i, j, there):
        return copy_to(
            sources[i].at[:, cols(there, j)],
            in_buf.at[j, i, first[i] + x],
            in_send,
            in_recv.at[j],
            (s, there),
        )

    def in_local(i, j):
        return pltpu.make_async_copy(
            sources[i].at[:, cols(x, j)], in_buf.at[j, i, first[i] + x], in_local_sem.at[j]
        )

    def stat_copy(there):
        return copy_to(own_stats.at[there], stats.at[x], stat_send, stat_recv, (s, there))

    def halo_copies(j):
        to_after = [
            copy_to(
                in_buf.at[j, i, pl.ds(RING, HALO)],
                in_buf.at[j, i, pl.ds(0, HALO)],
                halo_send,
                halo_recv.at[j],
                (after, x),
            )
            for i in (0, 1)
        ]
        to_before = [
            copy_to(
                in_buf.at[j, i, pl.ds(0, HALO)],
                in_buf.at[j, i, pl.ds(RING, HALO)],
                halo_send,
                halo_recv.at[j],
                (before, x),
            )
            for i in (2, 3)
        ]
        return to_after + to_before

    stat_halo = copy_to(
        stats.at[pl.ds(0, HALO)],
        stats.at[pl.ds(RING, HALO)],
        stat_halo_send,
        stat_halo_recv,
        (before, x),
    )

    def out_copy(i, j, there):
        return copy_to(
            out_buf.at[j, i, there],
            outs[i].at[:, cols(x, j)],
            out_send,
            out_recv,
            (s, there),
        )

    def out_local(i, j):
        return pltpu.make_async_copy(
            out_buf.at[j, i, x], outs[i].at[:, cols(x, j)], out_local_sem
        )

    for d in range(1, RING):
        stat_copy(lax.rem(x + d, RING)).start()

    def send_inputs(j, carry):
        for d in (2, 1, 3):
            for i in range(4):
                in_copy(i, j, lax.rem(x + d, RING)).start()
        for i in range(4):
            in_local(i, j).start()
        return carry

    lax.fori_loop(0, per, send_inputs, 0)
    stats[x] = own_stats[x]
    covers(stats.at[pl.ds(0, RING - 1)], stat_send, stat_recv).wait_recv()
    stat_halo.start()

    def compute(j):
        row = lax.broadcasted_iota(jnp.int32, (BLK, BLK), 0)
        col = lax.broadcasted_iota(jnp.int32, (BLK, BLK), 1)
        causal = col >= row
        for a in range(RING + HALO):
            low = max(a - HALO, 0)
            high = a + 1
            blocks = high - low
            keys = in_buf[j, 0, a]
            values = in_buf[j, 1, a]
            queries = in_buf[j, 2, low:high].reshape(blocks * BLK, DIM)
            grads = in_buf[j, 3, low:high].reshape(blocks * BLK, DIM)
            scores = dot(keys, queries, NT)
            dprobs = dot(values, grads, NT)
            halves, dscores = [], []
            for n in range(blocks):
                b = low + n
                distance = b - (a - HALO)
                distance = -distance if distance < 0 else distance
                tile = slice(n * BLK, (n + 1) * BLK)
                gap = b + HALO - a
                lse = stats[b, pl.ds(j, 1), :]
                delta = stats[b, pl.ds(per + j, 1), :]
                count = stats[b, 2 * per : 2 * per + 1, :]
                lse = jnp.where(count > gap, lse, NEVER)
                prob = jnp.exp2(scores[:, tile] * (scale * LOG2E) - lse)
                if gap == 0:
                    prob = jnp.where(causal, prob, 0.0)
                dscore = (prob * (dprobs[:, tile] - delta) * scale).astype(jnp.bfloat16)
                if b < RING:
                    ds_buf[b, (a - b) * BLK : (a - b + 1) * BLK, :] = dscore
                if a >= HALO:
                    halves.append(prob.astype(jnp.bfloat16))
                    dscores.append(dscore)
            if a >= HALO:
                half = jnp.concatenate(halves, axis=1)
                dscore = jnp.concatenate(dscores, axis=1)
                out_buf[j, 1, a - HALO] = dot(dscore, queries).astype(jnp.bfloat16)
                out_buf[j, 2, a - HALO] = dot(half, grads).astype(jnp.bfloat16)
        for b in range(RING):
            keys = in_buf[j, 0, b : b + RING].reshape(RING * BLK, DIM)
            out_buf[j, 0, b] = dot(ds_buf[b], keys, TN).astype(jnp.bfloat16)

    def step(j, carry):
        @pl.when(j < per)
        def _():
            covers(in_buf.at[j, :, pl.ds(0, RING - 1)], in_send, in_recv.at[j]).wait_recv()
            here = in_buf.at[j, :, 0]
            pltpu.make_async_copy(here, here, in_local_sem.at[j]).wait()
            for copy in halo_copies(j):
                copy.start()

        @pl.when(j > 0)
        def _():
            i = j - 1

            @pl.when(i == 0)
            def _():
                stat_halo.wait_recv()

            covers(in_buf.at[i, :, pl.ds(0, HALO)], halo_send, halo_recv.at[i]).wait_recv()
            compute(i)
            for d in (2, 1, 3):
                for n in range(3):
                    out_copy(n, i, lax.rem(x + d, RING)).start()
            for n in range(3):
                out_local(n, i).start()

        return carry

    lax.fori_loop(0, per + 1, step, 0)

    covers(stats.at[pl.ds(0, RING - 1)], stat_send, stat_recv).wait_send()
    stat_halo.wait_send()
    inputs = in_buf.at[:, :, pl.ds(0, RING - 1)]
    covers(inputs, in_send, in_recv.at[0]).wait_send()
    covers(inputs, halo_send, halo_recv.at[0]).wait_send()
    results = out_buf.at[:, :, pl.ds(0, RING - 1)]
    covers(results, out_send, out_recv).wait_send()
    covers(results, out_send, out_recv).wait_recv()
    own = out_buf.at[:, :, 0]
    pltpu.make_async_copy(own, own, out_local_sem).wait()


def shards(groups, q, k, v, g, lse, delta, counts):
    heads = lse.shape[0]
    per = heads // RING
    rows, width = q.shape
    hbm = pl.BlockSpec(memory_space=pl.ANY)
    vmem = pl.BlockSpec(memory_space=pltpu.VMEM)
    grad = jax.ShapeDtypeStruct((rows, width), jnp.bfloat16)
    return pl.pallas_call(
        functools.partial(kernel, groups, per),
        out_shape=(grad, grad, grad),
        in_specs=[hbm] * 4 + [vmem] * 2 + [pl.BlockSpec(memory_space=pltpu.SMEM)],
        out_specs=(hbm, hbm, hbm),
        scratch_shapes=[
            pltpu.VMEM((per, 4, RING + HALO, BLK, DIM), jnp.bfloat16),
            pltpu.VMEM((RING, 16, BLK), jnp.float32),
            pltpu.VMEM((RING + HALO, 16, BLK), jnp.float32),
            pltpu.VMEM((per, 3, RING, BLK, DIM), jnp.bfloat16),
            pltpu.VMEM((RING, RING * BLK, BLK), jnp.bfloat16),
            pltpu.SemaphoreType.DMA,
            pltpu.SemaphoreType.DMA((per,)),
            pltpu.SemaphoreType.DMA((per,)),
            pltpu.SemaphoreType.DMA,
            pltpu.SemaphoreType.DMA((per,)),
            pltpu.SemaphoreType.DMA,
            pltpu.SemaphoreType.DMA,
            pltpu.SemaphoreType.DMA,
            pltpu.SemaphoreType.DMA,
            pltpu.SemaphoreType.DMA,
            pltpu.SemaphoreType.DMA,
            pltpu.SemaphoreType.DMA,
        ],
        compiler_params=pltpu.CompilerParams(
            collective_id=0, has_side_effects=True, vmem_limit_bytes=40 << 20
        ),
        cost_estimate=pl.CostEstimate(
            flops=184 * per * BLK * BLK * DIM,
            bytes_accessed=14 * rows * width,
            transcendentals=22 * per * BLK * BLK,
        ),
    )(q, k, v, g, lse, delta, counts)


def solution(mesh):
    groups = mesh.shape["seq"]
    rows = P(("seq", "pair"), None)
    cols = P(None, ("seq", "pair"))
    return jax.shard_map(
        functools.partial(shards, groups),
        mesh=mesh,
        in_specs=(rows, rows, rows, rows, cols, cols, P(("seq", "pair"))),
        out_specs=(rows, rows, rows),
        check_vma=False,
    )
```

```python
import functools
import math

import jax
import jax.numpy as jnp
from jax import lax
from jax.experimental import pallas as pl
from jax.experimental.pallas import tpu as pltpu
from jax.sharding import PartitionSpec as P

MESH = pl.DeviceIdType.MESH
BLK = 128
DIM = 128
RING = 4
HALO = 3
LOG2E = math.log2(math.e)
NEVER = 1e30
NT = (((1,), (1,)), ((), ()))
TN = (((0,), (0,)), ((), ()))


def dot(a, b, dims=(((1,), (0,)), ((), ()))):
    return lax.dot_general(a, b, dims, preferred_element_type=jnp.float32)


def kernel(
    groups,
    per,
    q_hbm,
    k_hbm,
    v_hbm,
    g_hbm,
    lse_hbm,
    delta_hbm,
    cnt_ref,
    dq_hbm,
    dk_hbm,
    dv_hbm,
    lse_ref,
    delta_ref,
    q_ref,
    k_ref,
    v_ref,
    g_ref,
    in_buf,
    own_stats,
    stats,
    out_buf,
    ds_buf,
    in_send,
    in_recv,
    in_local_sem,
    halo_send,
    halo_recv,
    stat_send,
    stat_recv,
    stat_halo_send,
    stat_halo_recv,
    out_send,
    out_recv,
    out_local_sem,
    row_sem,
):
    s = lax.axis_index("seq")
    x = lax.axis_index("pair")
    after = lax.rem(s + 1, groups)
    before = lax.rem(s + groups - 1, groups)
    scale = DIM ** (-0.5)

    fetches = [
        pltpu.make_async_copy(lse_hbm, lse_ref, row_sem.at[0]),
        pltpu.make_async_copy(delta_hbm, delta_ref, row_sem.at[1]),
        pltpu.make_async_copy(k_hbm, k_ref, row_sem.at[2]),
        pltpu.make_async_copy(v_hbm, v_ref, row_sem.at[3]),
        pltpu.make_async_copy(q_hbm, q_ref, row_sem.at[4]),
        pltpu.make_async_copy(g_hbm, g_ref, row_sem.at[5]),
    ]
    for fetch in fetches:
        fetch.start()

    barrier = pltpu.get_barrier_semaphore()
    for d in range(1, RING):
        pl.semaphore_signal(
            barrier, 1, device_id=(s, lax.rem(x + d, RING)), device_id_type=MESH
        )
    pl.semaphore_signal(barrier, 1, device_id=(after, x), device_id_type=MESH)
    pl.semaphore_signal(barrier, 1, device_id=(before, x), device_id_type=MESH)
    pl.semaphore_wait(barrier, RING + 1)

    def cols(owner, j):
        return pl.ds(pl.multiple_of((owner * per + j) * DIM, DIM), DIM)

    sources = (k_ref, v_ref, q_ref, g_ref)
    first = (HALO, HALO, 0, 0)
    outs = (dq_hbm, dk_hbm, dv_hbm)

    def copy_to(src, dst, send, recv, device):
        return pltpu.make_async_remote_copy(
            src_ref=src,
            dst_ref=dst,
            send_sem=send,
            recv_sem=recv,
            device_id=device,
            device_id_type=MESH,
        )

    def covers(ref, send, recv):
        return copy_to(ref, ref, send, recv, (after, x))

    def in_copy(i, j, there):
        return copy_to(
            sources[i].at[:, cols(there, j)],
            in_buf.at[j, i, first[i] + x],
            in_send,
            in_recv.at[j],
            (s, there),
        )

    def in_local(i, j):
        return pltpu.make_async_copy(
            sources[i].at[:, cols(x, j)], in_buf.at[j, i, first[i] + x], in_local_sem.at[j]
        )

    def stat_copy(there):
        return copy_to(own_stats.at[there], stats.at[x], stat_send, stat_recv, (s, there))

    def halo_copies(j):
        to_after = [
            copy_to(
                in_buf.at[j, i, pl.ds(RING, HALO)],
                in_buf.at[j, i, pl.ds(0, HALO)],
                halo_send,
                halo_recv.at[j],
                (after, x),
            )
            for i in (0, 1)
        ]
        to_before = [
            copy_to(
                in_buf.at[j, i, pl.ds(0, HALO)],
                in_buf.at[j, i, pl.ds(RING, HALO)],
                halo_send,
                halo_recv.at[j],
                (before, x),
            )
            for i in (2, 3)
        ]
        return to_after + to_before

    stat_halo = copy_to(
        stats.at[pl.ds(0, HALO)],
        stats.at[pl.ds(RING, HALO)],
        stat_halo_send,
        stat_halo_recv,
        (before, x),
    )

    def out_copy(i, j, there):
        return copy_to(
            out_buf.at[j, i, there],
            outs[i].at[:, cols(x, j)],
            out_send,
            out_recv,
            (s, there),
        )

    def out_local(i, j):
        return pltpu.make_async_copy(
            out_buf.at[j, i, x], outs[i].at[:, cols(x, j)], out_local_sem
        )

    for fetch in fetches[:2]:
        fetch.wait()
    own_stats[...] = jnp.zeros_like(own_stats)
    for c in range(RING):
        own_stats[c, 0:per] = lse_ref[c * per : (c + 1) * per, :] * LOG2E
        own_stats[c, per : 2 * per] = delta_ref[c * per : (c + 1) * per, :]
        own_stats[c, 2 * per : 2 * per + 1] = jnp.full((1, BLK), cnt_ref[0], jnp.int32).astype(
            jnp.float32
        )
    for d in range(1, RING):
        stat_copy(lax.rem(x + d, RING)).start()
    stats[x] = own_stats[x]

    for fetch in fetches[2:]:
        fetch.wait()

    def send_inputs(j, carry):
        for d in (2, 1, 3):
            for i in range(4):
                in_copy(i, j, lax.rem(x + d, RING)).start()
        for i in range(4):
            in_local(i, j).start()
        return carry

    lax.fori_loop(0, per, send_inputs, 0)
    covers(stats.at[pl.ds(0, RING - 1)], stat_send, stat_recv).wait_recv()
    stat_halo.start()

    def compute(j):
        row = lax.broadcasted_iota(jnp.int32, (BLK, BLK), 0)
        col = lax.broadcasted_iota(jnp.int32, (BLK, BLK), 1)
        causal = col >= row
        for a in range(RING + HALO):
            low = max(a - HALO, 0)
            high = a + 1
            blocks = high - low
            keys = in_buf[j, 0, a]
            values = in_buf[j, 1, a]
            queries = in_buf[j, 2, low:high].reshape(blocks * BLK, DIM)
            grads = in_buf[j, 3, low:high].reshape(blocks * BLK, DIM)
            scores = dot(keys, queries, NT)
            dprobs = dot(values, grads, NT)
            halves, dscores = [], []
            for n in range(blocks):
                b = low + n
                distance = b - (a - HALO)
                distance = -distance if distance < 0 else distance
                tile = slice(n * BLK, (n + 1) * BLK)
                gap = b + HALO - a
                lse = stats[b, pl.ds(j, 1), :]
                delta = stats[b, pl.ds(per + j, 1), :]
                count = stats[b, 2 * per : 2 * per + 1, :]
                lse = jnp.where(count > gap, lse, NEVER)
                prob = jnp.exp2(scores[:, tile] * (scale * LOG2E) - lse)
                if gap == 0:
                    prob = jnp.where(causal, prob, 0.0)
                dscore = (prob * (dprobs[:, tile] - delta) * scale).astype(jnp.bfloat16)
                if b < RING:
                    ds_buf[b, (a - b) * BLK : (a - b + 1) * BLK, :] = dscore
                if a >= HALO:
                    halves.append(prob.astype(jnp.bfloat16))
                    dscores.append(dscore)
            if a >= HALO:
                half = jnp.concatenate(halves, axis=1)
                dscore = jnp.concatenate(dscores, axis=1)
                out_buf[j, 1, a - HALO] = dot(dscore, queries).astype(jnp.bfloat16)
                out_buf[j, 2, a - HALO] = dot(half, grads).astype(jnp.bfloat16)
        for b in range(RING):
            keys = in_buf[j, 0, b : b + RING].reshape(RING * BLK, DIM)
            out_buf[j, 0, b] = dot(ds_buf[b], keys, TN).astype(jnp.bfloat16)

    def step(j, carry):
        @pl.when(j < per)
        def _():
            covers(in_buf.at[j, :, pl.ds(0, RING - 1)], in_send, in_recv.at[j]).wait_recv()
            here = in_buf.at[j, :, 0]
            pltpu.make_async_copy(here, here, in_local_sem.at[j]).wait()
            for copy in halo_copies(j):
                copy.start()

        @pl.when(j > 0)
        def _():
            i = j - 1

            @pl.when(i == 0)
            def _():
                stat_halo.wait_recv()

            covers(in_buf.at[i, :, pl.ds(0, HALO)], halo_send, halo_recv.at[i]).wait_recv()
            compute(i)
            for d in (2, 1, 3):
                for n in range(3):
                    out_copy(n, i, lax.rem(x + d, RING)).start()
            for n in range(3):
                out_local(n, i).start()

        return carry

    lax.fori_loop(0, per + 1, step, 0)

    covers(stats.at[pl.ds(0, RING - 1)], stat_send, stat_recv).wait_send()
    stat_halo.wait_send()
    inputs = in_buf.at[:, :, pl.ds(0, RING - 1)]
    covers(inputs, in_send, in_recv.at[0]).wait_send()
    covers(inputs, halo_send, halo_recv.at[0]).wait_send()
    results = out_buf.at[:, :, pl.ds(0, RING - 1)]
    covers(results, out_send, out_recv).wait_send()
    covers(results, out_send, out_recv).wait_recv()
    own = out_buf.at[:, :, 0]
    pltpu.make_async_copy(own, own, out_local_sem).wait()


def keep(a, b, c, a_out, b_out, c_out, sems):
    copies = [
        pltpu.make_async_copy(src, dst, sems.at[i])
        for i, (src, dst) in enumerate(((a, a_out), (b, b_out), (c, c_out)))
    ]
    for copy in copies:
        copy.start()
    for copy in copies:
        copy.wait()


def shards(groups, q, k, v, g, lse, delta, counts):
    heads = lse.shape[0]
    per = heads // RING
    rows, width = q.shape
    hbm = pl.BlockSpec(memory_space=pl.ANY)
    vmem = pl.BlockSpec(memory_space=pltpu.VMEM)
    grad = jax.ShapeDtypeStruct((rows, width), jnp.bfloat16)
    grads = pl.pallas_call(
        functools.partial(kernel, groups, per),
        out_shape=(grad, grad, grad),
        in_specs=[hbm] * 6 + [pl.BlockSpec(memory_space=pltpu.SMEM)],
        out_specs=(vmem, vmem, vmem),
        scratch_shapes=[
            pltpu.VMEM(lse.shape, jnp.float32),
            pltpu.VMEM(delta.shape, jnp.float32),
            pltpu.VMEM((rows, width), jnp.bfloat16),
            pltpu.VMEM((rows, width), jnp.bfloat16),
            pltpu.VMEM((rows, width), jnp.bfloat16),
            pltpu.VMEM((rows, width), jnp.bfloat16),
            pltpu.VMEM((per, 4, RING + HALO, BLK, DIM), jnp.bfloat16),
            pltpu.VMEM((RING, 16, BLK), jnp.float32),
            pltpu.VMEM((RING + HALO, 16, BLK), jnp.float32),
            pltpu.VMEM((per, 3, RING, BLK, DIM), jnp.bfloat16),
            pltpu.VMEM((RING, RING * BLK, BLK), jnp.bfloat16),
            pltpu.SemaphoreType.DMA,
            pltpu.SemaphoreType.DMA((per,)),
            pltpu.SemaphoreType.DMA((per,)),
            pltpu.SemaphoreType.DMA,
            pltpu.SemaphoreType.DMA((per,)),
            pltpu.SemaphoreType.DMA,
            pltpu.SemaphoreType.DMA,
            pltpu.SemaphoreType.DMA,
            pltpu.SemaphoreType.DMA,
            pltpu.SemaphoreType.DMA,
            pltpu.SemaphoreType.DMA,
            pltpu.SemaphoreType.DMA,
            pltpu.SemaphoreType.DMA((6,)),
        ],
        compiler_params=pltpu.CompilerParams(
            collective_id=0, has_side_effects=True, vmem_limit_bytes=123 << 19
        ),
        cost_estimate=pl.CostEstimate(
            flops=184 * per * BLK * BLK * DIM,
            bytes_accessed=14 * rows * width,
            transcendentals=22 * per * BLK * BLK,
        ),
    )(q, k, v, g, lse, delta, counts)
    return pl.pallas_call(
        keep,
        out_shape=(grad, grad, grad),
        in_specs=[vmem] * 3,
        out_specs=(hbm, hbm, hbm),
        scratch_shapes=[pltpu.SemaphoreType.DMA((3,))],
        cost_estimate=pl.CostEstimate(
            flops=0, bytes_accessed=6 * rows * width, transcendentals=0
        ),
    )(*grads)


def solution(mesh):
    groups = mesh.shape["seq"]
    rows = P(("seq", "pair"), None)
    cols = P(None, ("seq", "pair"))
    return jax.shard_map(
        functools.partial(shards, groups),
        mesh=mesh,
        in_specs=(rows, rows, rows, rows, cols, cols, P(("seq", "pair"))),
        out_specs=(rows, rows, rows),
        check_vma=False,
    )
```

```python
import functools
import math

import jax
import jax.numpy as jnp
from jax import lax
from jax.experimental import pallas as pl
from jax.experimental.pallas import tpu as pltpu
from jax.sharding import PartitionSpec as P

MESH = pl.DeviceIdType.MESH
BLK = 128
DIM = 128
RING = 4
LOG2E = math.log2(math.e)
NEVER = 1e30
NN = (((1,), (0,)), ((), ()))
NT = (((1,), (1,)), ((), ()))
TN = (((0,), (0,)), ((), ()))
FWD, BACK = 4, 5


def dot(a, b, dims=NN):
    return lax.dot_general(a, b, dims, preferred_element_type=jnp.float32)


def either(flags):
    total = flags[0]
    for flag in flags[1:]:
        total = jnp.logical_or(total, flag)
    return total


def both(a, b):
    return jnp.logical_and(a, b)


def kernel(
    blocks,
    heads,
    q_hbm,
    k_hbm,
    v_hbm,
    g_hbm,
    lse_hbm,
    delta_hbm,
    cnt_ref,
    dq_ref,
    dk_ref,
    dv_ref,
    q_own,
    k_own,
    v_own,
    g_own,
    kv_far,
    qg_far,
    stats,
    counts,
    send_f,
    send_b,
    got_f,
    got_b,
    far_f,
    far_b,
    acc,
    part,
    fetch_sem,
    count_send,
    count_recv,
    stat_send,
    stat_recv,
    pre_send,
    pre_recv,
    f_send,
    f_recv,
    b_send,
    b_recv,
    far_send,
    far_recv,
):
    periods = heads // 4
    x = lax.axis_index("pair")
    me = lax.axis_index("seq") * RING + x
    scale = DIM ** (-0.5)

    def at(offset):
        there = lax.rem(me + (offset + blocks), blocks)
        return (lax.div(there, RING), lax.rem(there, RING))

    def remote(src, dst, send, recv, offset):
        return pltpu.make_async_remote_copy(
            src_ref=src,
            dst_ref=dst,
            send_sem=send,
            recv_sem=recv,
            device_id=at(offset),
            device_id_type=MESH,
        )

    fetches = [
        pltpu.make_async_copy(lse_hbm, stats.at[0, pl.ds(0, heads)], fetch_sem.at[0]),
        pltpu.make_async_copy(delta_hbm, stats.at[0, pl.ds(heads, heads)], fetch_sem.at[1]),
        pltpu.make_async_copy(k_hbm, k_own, fetch_sem.at[2]),
        pltpu.make_async_copy(v_hbm, v_own, fetch_sem.at[3]),
        pltpu.make_async_copy(q_hbm, q_own, fetch_sem.at[4]),
        pltpu.make_async_copy(g_hbm, g_own, fetch_sem.at[5]),
    ]
    for fetch in fetches:
        fetch.start()
    counts[0] = jnp.full((8, BLK), cnt_ref[0], jnp.int32).astype(jnp.float32)

    barrier = pltpu.get_barrier_semaphore()
    for offset in (-1, 1, 2, 3, -3, -4, 4):
        pl.semaphore_signal(barrier, 1, device_id=at(offset), device_id_type=MESH)
    pl.semaphore_wait(barrier, 7)

    count_copies = [
        remote(counts.at[0], counts.at[i], count_send.at[i], count_recv.at[i], -i)
        for i in (1, 2, 3)
    ]
    for copy in count_copies:
        copy.start()

    stat_copies = [
        remote(stats.at[0], stats.at[i], stat_send.at[i], stat_recv.at[i], offset)
        for i, offset in ((1, -1), (2, 1), (3, -3))
    ]

    for fetch in fetches[:2]:
        fetch.wait()
    for copy in stat_copies:
        copy.start()

    def wide(k, first):
        return pl.ds(pl.multiple_of((4 * k + first) * DIM, 2 * DIM), 2 * DIM)

    def pre_copy(i, k):
        own = (k_own, v_own, q_own, g_own)[i]
        src = own.at[:, wide(k, 0 if i < 2 else 2)]
        dst = (kv_far if i < 2 else qg_far).at[k, i % 2]
        return remote(src, dst, pre_send.at[i, k], pre_recv.at[i, k], 4 if i < 2 else -4)

    def start_pre(k):
        for i in range(4):
            pre_copy(i, k).start()

    for fetch in fetches[2:]:
        fetch.wait()
    start_pre(0)
    place = cnt_ref[0]
    p0, p1, p2, p3 = (place == i for i in (1, 2, 3, 4))

    def cols(k, i):
        return pl.ds(pl.multiple_of((4 * k + i) * DIM, DIM), DIM)

    def content(kind, i, k, side):
        if kind == "kv":
            return (k_own, v_own)[side][:, cols(k, i)]
        if kind == "qg":
            return (q_own, g_own)[side][:, cols(k, i)]
        if kind == "kvx":
            return kv_far[k, side, :, i * DIM : (i + 1) * DIM]
        if kind == "qgx":
            return qg_far[k, side, :, (i - 2) * DIM : (i - 1) * DIM]
        if kind == "dkv":
            return part[k - 1, i, 1 + side]
        return part[k - 1, i + side, 0]

    def fwd_copy(k, s):
        return remote(send_f.at[k, s], got_f.at[k, s], f_send.at[k, s], f_recv.at[k, s], 1)

    def back_copy(k, s):
        return remote(send_b.at[k, s], got_b.at[k, s], b_send.at[k, s], b_recv.at[k, s], -1)

    def far_copy(k, i):
        if i == 0:
            src, dst = got_f.at[k, pl.ds(2, 2)], far_f.at[k]
        else:
            src, dst = got_b.at[k, 4], far_b.at[k]
        return remote(src, dst, far_send.at[k, i], far_recv.at[k, i], -4 if i == 0 else 4)

    def direct_copy(i):
        if i == 0:
            src, dst = part.at[periods - 1, pl.ds(0, 2), pl.ds(1, 2)], far_f.at[periods]
        else:
            src, dst = part.at[periods - 1, pl.ds(2, 2), 0], far_b.at[periods]
        at_end = (far_send.at[periods, i], far_recv.at[periods, i])
        return remote(src, dst, *at_end, -3 if i == 0 else 3)

    def send(table, k, s, back, ins=True, outs=True):
        stage = send_b if back else send_f
        table = [e for e in table if (ins and e[1][0] != "d") or (outs and e[1][0] == "d")]
        for side in range(2):
            value = content(table[-1][1], table[-1][2], k, side)
            for flag, kind, i in table[:-1]:
                value = jnp.where(flag, content(kind, i, k, side), value)
            stage[k, s, side] = value
        (back_copy if back else fwd_copy)(k, s).start()

    def wait_pre(k, which):
        for i in which:
            pre_copy(i, k).wait_recv()

    send(((p1, "kv", 3), (None, "qg", 2)), 0, 2, True)
    send(((None, "qg", 3),), 0, 3, True)
    start_pre(1)
    wait_pre(0, (0, 1))
    for s in range(2):
        send(((p0, "kvx", s), (None, "qg", s)), 0, s, True)

    for copy in count_copies:
        copy.wait_recv()
    c1, c2, c3 = (jnp.max(counts[i]) for i in (1, 2, 3))
    p0l4 = both(p0, c3 == 4.0)
    p1l4 = both(p1, c2 == 4.0)
    p2l4 = both(p2, c1 == 4.0)
    p0s = both(both(p0, c1 == 2.0), c3 != 4.0)
    p1s = both(p1, c2 != 4.0)
    p1g3 = both(p1, c1 == 3.0)
    p1l3 = both(p1g3, c2 != 4.0)
    p2l3 = both(p2, c1 != 4.0)
    last = c1 == 1.0

    fwd_table = (
        ((p0l4, "kv", 2), (either([p0s, p1l4]), "kv", 0), (p2l4, "qg", 0), (last, "qgx", 2)),
        ((p0l4, "kv", 3), (either([p0s, p1l4]), "kv", 1), (p2l4, "qg", 1), (last, "qgx", 3)),
        (
            (either([p0s, p1l4]), "kv", 2),
            (either([p0l4, p1l3, p2l4]), "dq", 0),
            (p3, "dkv", 0),
        ),
        (
            (p0s, "kv", 3),
            (p0l4, "dkv", 3),
            (either([p1g3, p2l4]), "dq", 2),
            (p3, "dkv", 1),
        ),
    )
    back_table = (
        ((p0, "kvx", 0), (either([p2l4, p1s]), "dkv", 0), (None, "qg", 0)),
        ((p0, "kvx", 1), (either([p2l4, p1s]), "dkv", 1), (None, "qg", 1)),
        ((p1, "kv", 3), (None, "qg", 2)),
        ((p1, "dkv", 2), (None, "qg", 3)),
        ((p1, "dkv", 3), (p2l4, "dkv", 2), (p3, "dq", 0), (None, "dq", 2)),
    )

    def post(k, s, back, ins=True, outs=True):
        send((back_table if back else fwd_table)[s], k, s, back, ins, outs)

    row = lax.broadcasted_iota(jnp.int32, (BLK, BLK), 0)
    col = lax.broadcasted_iota(jnp.int32, (BLK, BLK), 1)
    causal = col >= row

    has_k = (either([p3, p2l4, p1s]),) * 2 + (either([p1, p2l4]), either([p0l4, p1]))
    has_q = (either([p0l4, p2l4, p3, p1l3]),) * 2 + (either([p0l4, p1g3, p2l4]),) * 2
    own_q_far_k = (has_k[0], has_k[1], p1, p1)
    far_q_own_k = (both(has_q[0], jnp.logical_not(p3)),) * 2 + (has_q[2], has_q[3])

    def compute(k, i):
        f = [got_f.at[k, s] for s in range(FWD)]
        b = [got_b.at[k, s] for s in range(BACK)]

        def far_kv(side):
            if i < 2:
                value = jnp.where(p3, b[i][side], f[i][side])
            elif i == 2:
                value = jnp.where(p1l4, f[0][side], f[2][side])
            else:
                value = jnp.where(p1l4, f[1][side], f[3][side])
                value = jnp.where(p0, b[2][side], value)
            return jnp.where(has_k[i], value, jnp.zeros_like(value))

        def far_qg(side):
            if i < 2:
                value = jnp.where(p3, f[i][side], b[i][side])
            else:
                value = jnp.where(p0, f[i - 2][side], b[i][side])
            return jnp.where(has_q[i], value, jnp.zeros_like(value))

        here = cols(k, i)
        keys = jnp.concatenate([k_own[:, here], far_kv(0)], axis=0)
        values = jnp.concatenate([v_own[:, here], far_kv(1)], axis=0)
        queries = jnp.concatenate([q_own[:, here], far_qg(0)], axis=0)
        grads = jnp.concatenate([g_own[:, here], far_qg(1)], axis=0)
        h = 4 * k + i
        lse_row, delta_row = pl.ds(h, 1), pl.ds(heads + h, 1)

        def far_row(at_row):
            if i < 2:
                return jnp.where(p3, stats[2, at_row, :], stats[1, at_row, :])
            return jnp.where(p0, stats[3, at_row, :], stats[1, at_row, :])

        lse = [stats[0, lse_row, :] * LOG2E, far_row(lse_row) * LOG2E]
        delta = [stats[0, delta_row, :], far_row(delta_row)]
        scores = dot(keys, queries, NT)
        dprobs = dot(values, grads, NT)
        halves, dscores = [], []
        for u in range(2):
            for t in range(2):
                shift = lse[t]
                if u or t:
                    allowed = (
                        both(has_k[i], has_q[i])
                        if u and t
                        else (own_q_far_k[i] if u else far_q_own_k[i])
                    )
                    shift = jnp.where(allowed, shift, jnp.full_like(shift, NEVER))
                tile = (slice(u * BLK, (u + 1) * BLK), slice(t * BLK, (t + 1) * BLK))
                prob = jnp.exp2(scores[tile] * (scale * LOG2E) - shift)
                if not (u or t):
                    prob = jnp.where(causal, prob, 0.0)
                halves.append(prob.astype(jnp.bfloat16))
                dscores.append((prob * (dprobs[tile] - delta[t]) * scale).astype(jnp.bfloat16))

        def square(tiles):
            return jnp.concatenate(
                [jnp.concatenate(tiles[:2], axis=1), jnp.concatenate(tiles[2:], axis=1)], axis=0
            )

        half, dscore = square(halves), square(dscores)
        for n, value in enumerate(
            (dot(dscore, keys, TN), dot(dscore, queries), dot(half, grads))
        ):
            acc[k, i, n] = value[:BLK]
            part[k, i, n] = value[BLK:].astype(jnp.bfloat16)

    def finish(k):
        f = [got_f.at[k + 1, s] for s in range(FWD)]
        b = [got_b.at[k + 1, s] for s in range(BACK)]
        back_f, back_b = far_f.at[k + 1], far_b.at[k + 1]

        def add(total, flag, value):
            value = value.astype(jnp.float32)
            return total + jnp.where(flag, value, jnp.zeros_like(value))

        p1l4_p2_p3 = either([p1l4, p2, p3])
        p2_p3 = either([p2, p3])
        p0g2_p1l4 = either([p0l4, p0s, p1l4])
        for i in range(4):
            here = cols(k, i)
            if i < 2:
                value = jnp.where(p2l4, b[4][i], f[2][i])
                total = add(acc[k, i, 0], p1l4_p2_p3, value)
            else:
                total = add(acc[k, i, 0], p2_p3, f[3][i - 2])
                total = add(total, p3, back_b[i - 2])
            dq_ref[:, here] = total.astype(jnp.bfloat16)
            for side, out in enumerate((dk_ref, dv_ref)):
                if i < 2:
                    value = jnp.where(p0l4, back_f[i, side], b[i][side])
                elif i == 2:
                    value = jnp.where(p1l4, b[4][side], b[3][side])
                else:
                    value = jnp.where(p1l4, f[3][side], b[4][side])
                out[:, here] = add(acc[k, i, 1 + side], p0g2_p1l4, value).astype(jnp.bfloat16)

    def period(k, final):
        ahead = k + 1
        if not final:
            post(ahead, 2, True)

            @pl.when(k < periods - 2)
            def _():
                start_pre(k + 2)

        fwd_copy(k, 0).wait_recv()
        back_copy(k, 0).wait_recv()
        compute(k, 0)
        if not final:
            wait_pre(ahead, range(4))
        post(ahead, 0, True, ins=not final)
        if not final:
            post(ahead, 0, False)
            post(ahead, 1, False)
        fwd_copy(k, 1).wait_recv()
        back_copy(k, 1).wait_recv()
        compute(k, 1)
        post(ahead, 1, True, ins=not final)
        post(ahead, 2, False, ins=not final)
        if final:
            direct_copy(0).start()
        fwd_copy(k, 2).wait_recv()
        back_copy(k, 2).wait_recv()
        compute(k, 2)
        if not final:
            post(ahead, 3, True)
        fwd_copy(k, 3).wait_recv()
        back_copy(k, 3).wait_recv()
        compute(k, 3)
        if final:
            direct_copy(1).start()
        post(ahead, 3, False, ins=not final)
        post(ahead, 4, True, ins=not final)
        if final:
            post(ahead, 3, True, ins=False)

    def forward_far(k):
        far_copy(k, 0).start()
        back_copy(k, 4).wait_recv()
        far_copy(k, 1).start()

    wait_pre(0, (2, 3))
    for s in range(4):
        post(0, s, False, outs=False)
    for copy in stat_copies:
        copy.wait_recv()

    def drain(k):
        for i in range(4):
            pre_copy(i, k).wait_send()
        for s in range(4):
            fwd_copy(k, s).wait_send()
            back_copy(k, s).wait_send()

        @pl.when(k > 0)
        def _():
            back_copy(k, 4).wait_send()
            for i in range(2):
                far_copy(k, i).wait_send()

    def step(k, carry):
        period(k, False)

        @pl.when(k > 0)
        def _():
            forward_far(k)
            drain(k - 1)

        @pl.when(k > 1)
        def _():
            for i in range(2):
                far_copy(k - 1, i).wait_recv()
            finish(k - 2)

        return carry

    lax.fori_loop(0, periods - 1, step, 0)
    end = periods - 1
    period(end, True)
    forward_far(end)
    for i in range(2):
        far_copy(end - 1, i).wait_recv()
    finish(end - 2)
    drain(end - 1)
    drain(end)
    for copy in count_copies + stat_copies:
        copy.wait_send()
    for i in range(2):
        far_copy(end, i).wait_recv()
    finish(end - 1)
    for s in (2, 3):
        fwd_copy(periods, s).wait_recv()
    for s in (0, 1, 3, 4):
        back_copy(periods, s).wait_recv()
    for i in range(2):
        direct_copy(i).wait_recv()
    finish(end)
    for s in (2, 3):
        fwd_copy(periods, s).wait_send()
    for s in (0, 1, 3, 4):
        back_copy(periods, s).wait_send()
    for i in range(2):
        direct_copy(i).wait_send()


def keep(a, b, c, a_out, b_out, c_out, sems):
    copies = [
        pltpu.make_async_copy(src, dst, sems.at[i])
        for i, (src, dst) in enumerate(((a, a_out), (b, b_out), (c, c_out)))
    ]
    for copy in copies:
        copy.start()
    for copy in copies:
        copy.wait()


def shards(blocks, q, k, v, g, lse, delta, counts):
    heads = lse.shape[0]
    periods = heads // 4
    rows, width = q.shape
    hbm = pl.BlockSpec(memory_space=pl.ANY)
    vmem = pl.BlockSpec(memory_space=pltpu.VMEM)
    grad = jax.ShapeDtypeStruct((rows, width), jnp.bfloat16)
    dma = pltpu.SemaphoreType.DMA

    def tiles(*lead, dtype=jnp.bfloat16):
        return pltpu.VMEM((*lead, BLK, DIM), dtype)

    grads = pl.pallas_call(
        functools.partial(kernel, blocks, heads),
        out_shape=(grad, grad, grad),
        in_specs=[hbm] * 6 + [pl.BlockSpec(memory_space=pltpu.SMEM)],
        out_specs=(vmem, vmem, vmem),
        scratch_shapes=[
            pltpu.VMEM((rows, width), jnp.bfloat16),
            pltpu.VMEM((rows, width), jnp.bfloat16),
            pltpu.VMEM((rows, width), jnp.bfloat16),
            pltpu.VMEM((rows, width), jnp.bfloat16),
            pltpu.VMEM((periods, 2, BLK, 2 * DIM), jnp.bfloat16),
            pltpu.VMEM((periods, 2, BLK, 2 * DIM), jnp.bfloat16),
            pltpu.VMEM((4, 2 * heads, BLK), jnp.float32),
            pltpu.VMEM((4, 8, BLK), jnp.float32),
            tiles(periods + 1, FWD, 2),
            tiles(periods + 1, BACK, 2),
            tiles(periods + 1, FWD, 2),
            tiles(periods + 1, BACK, 2),
            tiles(periods + 1, 2, 2),
            tiles(periods + 1, 2),
            tiles(periods, 4, 3, dtype=jnp.float32),
            tiles(periods, 4, 3),
            dma((6,)),
            dma((4,)),
            dma((4,)),
            dma((4,)),
            dma((4,)),
            dma((4, periods)),
            dma((4, periods)),
            dma((periods + 1, FWD)),
            dma((periods + 1, FWD)),
            dma((periods + 1, BACK)),
            dma((periods + 1, BACK)),
            dma((periods + 1, 2)),
            dma((periods + 1, 2)),
        ],
        compiler_params=pltpu.CompilerParams(
            collective_id=0, has_side_effects=True, vmem_limit_bytes=123 << 19
        ),
        cost_estimate=pl.CostEstimate(
            flops=40 * heads * BLK * BLK * DIM,
            bytes_accessed=14 * rows * width,
            transcendentals=4 * heads * BLK * BLK,
        ),
    )(q, k, v, g, lse, delta, counts)
    return pl.pallas_call(
        keep,
        out_shape=(grad, grad, grad),
        in_specs=[vmem] * 3,
        out_specs=(hbm, hbm, hbm),
        scratch_shapes=[pltpu.SemaphoreType.DMA((3,))],
        cost_estimate=pl.CostEstimate(
            flops=0, bytes_accessed=6 * rows * width, transcendentals=0
        ),
    )(*grads)


def solution(mesh):
    blocks = mesh.shape["seq"] * mesh.shape["pair"]
    rows = P(("seq", "pair"), None)
    cols = P(None, ("seq", "pair"))
    return jax.shard_map(
        functools.partial(shards, blocks),
        mesh=mesh,
        in_specs=(rows, rows, rows, rows, cols, cols, P(("seq", "pair"))),
        out_specs=(rows, rows, rows),
        check_vma=False,
    )
```

```python
import functools
import math

import jax
import jax.numpy as jnp
from jax import lax
from jax.experimental import pallas as pl
from jax.experimental.pallas import tpu as pltpu
from jax.sharding import PartitionSpec as P

MESH = pl.DeviceIdType.MESH
BLK = 128
DIM = 128
RING = 4
LOG2E = math.log2(math.e)
NEVER = 1e30
NN = (((1,), (0,)), ((), ()))
NT = (((1,), (1,)), ((), ()))
TN = (((0,), (0,)), ((), ()))
FWD, BACK = 4, 5


def dot(a, b, dims=NN):
    return lax.dot_general(a, b, dims, preferred_element_type=jnp.float32)


def either(flags):
    total = flags[0]
    for flag in flags[1:]:
        total = jnp.logical_or(total, flag)
    return total


def both(a, b):
    return jnp.logical_and(a, b)


def kernel(
    blocks,
    heads,
    q_hbm,
    k_hbm,
    v_hbm,
    g_hbm,
    lse_hbm,
    delta_hbm,
    cnt_ref,
    dq_ref,
    dk_ref,
    dv_ref,
    q_own,
    k_own,
    v_own,
    g_own,
    kv_far,
    qg_far,
    stats,
    counts,
    send_f,
    send_b,
    got_f,
    got_b,
    far_f,
    far_b,
    acc,
    part,
    fetch_sem,
    count_send,
    count_recv,
    stat_send,
    stat_recv,
    pre_send,
    pre_recv,
    f_send,
    f_recv,
    b_send,
    b_recv,
    far_send,
    far_recv,
):
    periods = heads // 4
    x = lax.axis_index("pair")
    me = lax.axis_index("seq") * RING + x
    scale = DIM ** (-0.5)

    def at(offset):
        there = lax.rem(me + (offset + blocks), blocks)
        return (lax.div(there, RING), lax.rem(there, RING))

    def remote(src, dst, send, recv, offset):
        return pltpu.make_async_remote_copy(
            src_ref=src,
            dst_ref=dst,
            send_sem=send,
            recv_sem=recv,
            device_id=at(offset),
            device_id_type=MESH,
        )

    fetches = [
        pltpu.make_async_copy(lse_hbm, stats.at[0, pl.ds(0, heads)], fetch_sem.at[0]),
        pltpu.make_async_copy(delta_hbm, stats.at[0, pl.ds(heads, heads)], fetch_sem.at[1]),
    ]
    operands = ((q_hbm, q_own), (g_hbm, g_own), (k_hbm, k_own), (v_hbm, v_own))
    for n, columns in enumerate((pl.ds(0, 4 * DIM), pl.ds(4 * DIM, (heads - 4) * DIM))):
        fetches += [
            pltpu.make_async_copy(
                hbm.at[:, columns], own.at[:, columns], fetch_sem.at[2 + 4 * n + i]
            )
            for i, (hbm, own) in enumerate(operands)
        ]
    for fetch in fetches:
        fetch.start()
    counts[0] = jnp.full((8, BLK), cnt_ref[0], jnp.int32).astype(jnp.float32)
    counts[1:] = jnp.ones((3, 8, BLK), jnp.float32)

    def valid(offset):
        return me < blocks - offset if offset > 0 else me >= -offset

    def begin(copy, condition):
        pl.when(condition)(copy.start)

    def arrived(copy, condition):
        pl.when(condition)(copy.wait_recv)

    def sent(copy, condition):
        pl.when(condition)(copy.wait_send)

    at_first, at_third = me == 0, me == 3
    at_last, at_head, ahead_of_head = (me == blocks - i for i in (1, 4, 5))

    @pl.when(at_last)
    def _():
        stats[1] = jnp.zeros(stats.shape[1:], stats.dtype)

    barrier = pltpu.get_barrier_semaphore()
    for offset in (-1, 1, 2, 3, -3, -4, 4):

        @pl.when(valid(offset))
        def _(offset=offset):
            pl.semaphore_signal(barrier, 1, device_id=at(offset), device_id_type=MESH)

    near = {3: (0,), 4: (1, blocks - 1), 5: (2, blocks - 2, blocks - 3), 6: (3, blocks - 4)}
    for amount, places in near.items():

        @pl.when(either([me == place for place in places]))
        def _(amount=amount):
            pl.semaphore_wait(barrier, amount)

    @pl.when(both(me > 3, me < blocks - 4))
    def _():
        pl.semaphore_wait(barrier, 7)

    def cols(k, i):
        return pl.ds(pl.multiple_of((4 * k + i) * DIM, DIM), DIM)

    def wide(k, first):
        return pl.ds(pl.multiple_of((4 * k + first) * DIM, 2 * DIM), 2 * DIM)

    def pre_copy(i, k, early=False):
        own = ((k_hbm, v_hbm, q_hbm, g_hbm) if early else (k_own, v_own, q_own, g_own))[i]
        src = own.at[:, wide(k, 0 if i < 2 else 2)]
        dst = (kv_far if i < 2 else qg_far).at[k, i % 2]
        return remote(src, dst, pre_send.at[i, k], pre_recv.at[i, k], 4 if i < 2 else -4)

    def end_copies(i, k, early):
        own = ((k_hbm, v_hbm, q_hbm, g_hbm) if early else (k_own, v_own, q_own, g_own))[i]
        got, recv = (got_b, b_recv) if i < 2 else (got_f, f_recv)
        return [
            remote(
                own.at[:, cols(k, s if i < 2 else 2 + s)],
                got.at[k, s, i % 2],
                pre_send.at[i, k],
                recv.at[k, s],
                3 if i < 2 else -3,
            )
            for s in range(2)
        ]

    def start_pre(k, early=False):
        for i in range(4):
            begin(pre_copy(i, k, early), valid(4 if i < 2 else -4))
            for copy in end_copies(i, k, early):
                begin(copy, at_head if i < 2 else at_third)

    start_pre(0, True)

    count_copies = [
        remote(counts.at[0], counts.at[i], count_send.at[i], count_recv.at[i], -i)
        for i in (1, 2, 3)
    ]
    for i, copy in enumerate(count_copies):
        begin(copy, valid(-1 - i))

    stat_copies = [
        remote(stats.at[0], stats.at[i], stat_send.at[i], stat_recv.at[i], offset)
        for i, offset in ((1, -1), (2, 1), (3, -3))
    ]
    for fetch in fetches[:2]:
        fetch.wait()
    stat_offsets = (-1, 1, -3)
    for copy, offset in zip(stat_copies, stat_offsets):
        begin(copy, valid(offset))
    for fetch in fetches[2:6]:
        fetch.wait()
    place = cnt_ref[0]
    p0, p1, p2, p3 = (place == i for i in (1, 2, 3, 4))

    def content(kind, i, k, side):
        if kind == "kv":
            return (k_own, v_own)[side][:, cols(k, i)]
        if kind == "qg":
            return (q_own, g_own)[side][:, cols(k, i)]
        if kind == "kvx":
            return kv_far[k, side, :, i * DIM : (i + 1) * DIM]
        if kind == "qgx":
            return qg_far[k, side, :, (i - 2) * DIM : (i - 1) * DIM]
        if kind == "dkv":
            return part[k - 1, i, 1 + side]
        return part[k - 1, i + side, 0]

    def fwd_copy(k, s):
        return remote(send_f.at[k, s], got_f.at[k, s], f_send.at[k, s], f_recv.at[k, s], 1)

    def back_copy(k, s):
        return remote(send_b.at[k, s], got_b.at[k, s], b_send.at[k, s], b_recv.at[k, s], -1)

    def far_copy(k, i):
        if i == 0:
            src, dst = got_f.at[k, pl.ds(2, 2)], far_f.at[k]
        else:
            src, dst = got_b.at[k, 4], far_b.at[k]
        return remote(src, dst, far_send.at[k, i], far_recv.at[k, i], -4 if i == 0 else 4)

    def direct_copy(i):
        if i == 0:
            src, dst = part.at[periods - 1, pl.ds(0, 2), pl.ds(1, 2)], far_f.at[periods]
        else:
            src, dst = part.at[periods - 1, pl.ds(2, 2), 0], far_b.at[periods]
        at_end = (far_send.at[periods, i], far_recv.at[periods, i])
        return remote(src, dst, *at_end, -3 if i == 0 else 3)

    def end_far(k, i):
        if i == 0:
            src, dst = part.at[k - 1, pl.ds(0, 2), pl.ds(1, 2)], far_f.at[k]
        else:
            src, dst = part.at[k - 1, pl.ds(2, 2), 0], far_b.at[k]
        send_sem = (f_send if i == 0 else b_send).at[k, 0]
        return remote(src, dst, send_sem, far_recv.at[k, i], -3 if i == 0 else 3)

    def sends_f():
        return me < blocks - 1

    def sends_b(s):
        return both(me > 0, me != blocks - 4) if s in (2, 3) else me > 0

    def wait_f(k, s):
        arrived(fwd_copy(k, s), me > 0) if s in (2, 3) else fwd_copy(k, s).wait_recv()

    def wait_b(k, s, flush=False):
        if s in (2, 3):
            arrived(back_copy(k, s), both(me < blocks - 1, me != blocks - 5))
        elif s == 4 or flush:
            arrived(back_copy(k, s), me < blocks - 1)
        else:
            back_copy(k, s).wait_recv()

    def start_far(k, i):
        begin(far_copy(k, i), valid((-4, 4)[i]))
        begin(end_far(k, i), (at_last, at_first)[i])

    def wait_far(k, i):
        arrived(far_copy(k, i), (me < blocks - 3, me >= 3)[i])

    def send(table, k, s, back, ins=True, outs=True):
        stage = send_b if back else send_f
        table = [e for e in table if (ins and e[1][0] != "d") or (outs and e[1][0] == "d")]
        for side in range(2):
            value = content(table[-1][1], table[-1][2], k, side)
            for flag, kind, i in table[:-1]:
                value = jnp.where(flag, content(kind, i, k, side), value)
            stage[k, s, side] = value
        begin((back_copy if back else fwd_copy)(k, s), sends_b(s) if back else sends_f())

    def wait_pre(k, which):
        for i in which:
            arrived(pre_copy(i, k), valid(-4 if i < 2 else 4))

    def send_2(k):
        send(((p1, "kv", 3), (None, "qg", 2)), k, 2, True)

    send_2(0)
    send(((None, "qg", 3),), 0, 3, True)
    for fetch in fetches[6:]:
        fetch.wait()
    send_2(1)
    start_pre(1)
    for i, copy in enumerate(count_copies):
        arrived(copy, valid(1 + i))
    c1, c2, c3 = (jnp.max(counts[i]) for i in (1, 2, 3))
    p0l4 = both(p0, c3 == 4.0)
    p1l4 = both(p1, c2 == 4.0)
    p2l4 = both(p2, c1 == 4.0)
    p0s = both(both(p0, c1 == 2.0), c3 != 4.0)
    p1s = both(p1, c2 != 4.0)
    p1g3 = both(p1, c1 == 3.0)
    p1l3 = both(p1g3, c2 != 4.0)
    p2l3 = both(p2, c1 != 4.0)
    last = c1 == 1.0

    fwd_table = (
        ((p0l4, "kv", 2), (either([p0s, p1l4]), "kv", 0), (p2l4, "qg", 0), (last, "qgx", 2)),
        ((p0l4, "kv", 3), (either([p0s, p1l4]), "kv", 1), (p2l4, "qg", 1), (last, "qgx", 3)),
        (
            (either([p0s, p1l4]), "kv", 2),
            (either([p0l4, p1l3, p2l4]), "dq", 0),
            (p3, "dkv", 0),
        ),
        (
            (p0s, "kv", 3),
            (p0l4, "dkv", 3),
            (either([p1g3, p2l4]), "dq", 2),
            (p3, "dkv", 1),
        ),
    )
    back_table = (
        ((p0, "kvx", 0), (either([p2l4, p1s]), "dkv", 0), (None, "qg", 0)),
        ((p0, "kvx", 1), (either([p2l4, p1s]), "dkv", 1), (None, "qg", 1)),
        ((p1, "kv", 3), (None, "qg", 2)),
        ((p1, "dkv", 2), (None, "qg", 3)),
        ((p1, "dkv", 3), (p2l4, "dkv", 2), (p3, "dq", 0), (None, "dq", 2)),
    )

    def post(k, s, back, ins=True, outs=True):
        send((back_table if back else fwd_table)[s], k, s, back, ins, outs)

    row = lax.broadcasted_iota(jnp.int32, (BLK, BLK), 0)
    col = lax.broadcasted_iota(jnp.int32, (BLK, BLK), 1)
    causal = col >= row

    has_k = (either([p3, p2l4, p1s]),) * 2 + (either([p1, p2l4]), either([p0l4, p1]))
    has_q = (either([p0l4, p2l4, p3, p1l3]),) * 2 + (either([p0l4, p1g3, p2l4]),) * 2
    own_q_far_k = (has_k[0], has_k[1], p1, p1)
    far_q_own_k = (both(has_q[0], jnp.logical_not(p3)),) * 2 + (has_q[2], has_q[3])

    def compute(k, i):
        f = [got_f.at[k, s] for s in range(FWD)]
        b = [got_b.at[k, s] for s in range(BACK)]

        def far_kv(side):
            if i < 2:
                value = jnp.where(p3, b[i][side], f[i][side])
            elif i == 2:
                value = jnp.where(p1l4, f[0][side], f[2][side])
            else:
                value = jnp.where(p1l4, f[1][side], f[3][side])
                value = jnp.where(p0, b[2][side], value)
            return jnp.where(has_k[i], value, jnp.zeros_like(value))

        def far_qg(side):
            if i < 2:
                value = jnp.where(p3, f[i][side], b[i][side])
            else:
                value = jnp.where(p0, f[i - 2][side], b[i][side])
            return jnp.where(has_q[i], value, jnp.zeros_like(value))

        here = cols(k, i)
        keys = jnp.concatenate([k_own[:, here], far_kv(0)], axis=0)
        values = jnp.concatenate([v_own[:, here], far_kv(1)], axis=0)
        queries = jnp.concatenate([q_own[:, here], far_qg(0)], axis=0)
        grads = jnp.concatenate([g_own[:, here], far_qg(1)], axis=0)
        h = 4 * k + i
        lse_row, delta_row = pl.ds(h, 1), pl.ds(heads + h, 1)

        def far_row(at_row):
            if i < 2:
                return jnp.where(p3, stats[2, at_row, :], stats[1, at_row, :])
            return jnp.where(p0, stats[3, at_row, :], stats[1, at_row, :])

        lse = [stats[0, lse_row, :] * LOG2E, far_row(lse_row) * LOG2E]
        delta = [stats[0, delta_row, :], far_row(delta_row)]
        scores = dot(keys, queries, NT)
        dprobs = dot(values, grads, NT)
        halves, dscores = [], []
        for u in range(2):
            for t in range(2):
                shift = lse[t]
                if u or t:
                    allowed = (
                        both(has_k[i], has_q[i])
                        if u and t
                        else (own_q_far_k[i] if u else far_q_own_k[i])
                    )
                    shift = jnp.where(allowed, shift, jnp.full_like(shift, NEVER))
                tile = (slice(u * BLK, (u + 1) * BLK), slice(t * BLK, (t + 1) * BLK))
                prob = jnp.exp2(scores[tile] * (scale * LOG2E) - shift)
                if not (u or t):
                    prob = jnp.where(causal, prob, 0.0)
                halves.append(prob.astype(jnp.bfloat16))
                dscores.append((prob * (dprobs[tile] - delta[t]) * scale).astype(jnp.bfloat16))

        def square(tiles):
            return jnp.concatenate(
                [jnp.concatenate(tiles[:2], axis=1), jnp.concatenate(tiles[2:], axis=1)], axis=0
            )

        half, dscore = square(halves), square(dscores)
        for n, value in enumerate(
            (dot(dscore, keys, TN), dot(dscore, queries), dot(half, grads))
        ):
            acc[k, i, n] = value[:BLK]
            part[k, i, n] = value[BLK:].astype(jnp.bfloat16)

    def finish(k):
        f = [got_f.at[k + 1, s] for s in range(FWD)]
        b = [got_b.at[k + 1, s] for s in range(BACK)]
        back_f, back_b = far_f.at[k + 1], far_b.at[k + 1]

        def add(total, flag, value):
            value = value.astype(jnp.float32)
            return total + jnp.where(flag, value, jnp.zeros_like(value))

        p1l4_p2_p3 = either([p1l4, p2, p3])
        p2_p3 = either([p2, p3])
        p0g2_p1l4 = either([p0l4, p0s, p1l4])
        for i in range(4):
            here = cols(k, i)
            if i < 2:
                value = jnp.where(p2l4, b[4][i], f[2][i])
                total = add(acc[k, i, 0], p1l4_p2_p3, value)
            else:
                total = add(acc[k, i, 0], p2_p3, f[3][i - 2])
                total = add(total, p3, back_b[i - 2])
            dq_ref[:, here] = total.astype(jnp.bfloat16)
            for side, out in enumerate((dk_ref, dv_ref)):
                if i < 2:
                    value = jnp.where(p0l4, back_f[i, side], b[i][side])
                elif i == 2:
                    value = jnp.where(p1l4, b[4][side], b[3][side])
                else:
                    value = jnp.where(p1l4, f[3][side], b[4][side])
                out[:, here] = add(acc[k, i, 1 + side], p0g2_p1l4, value).astype(jnp.bfloat16)

    def forward_back(k):
        wait_b(k, 4)
        start_far(k, 1)

    def period(k, final):
        ahead = k + 1
        if not final:

            @pl.when(k < periods - 3)
            def _():
                start_pre(k + 3)

        wait_f(k, 0)
        wait_b(k, 0)
        compute(k, 0)
        if not final:
            wait_pre(ahead, (0, 1))
        post(ahead, 0, True, ins=not final)
        wait_f(k, 1)
        wait_b(k, 1)
        compute(k, 1)
        post(ahead, 1, True, ins=not final)
        post(ahead, 2, False, ins=not final)
        if final:
            begin(direct_copy(0), valid(-3))

        @pl.when(k > 1)
        def _():
            forward_back(k - 1)

        wait_f(k, 2)
        wait_b(k, 2)
        compute(k, 2)
        if not final:
            post(ahead, 3, True)

            @pl.when(k < periods - 2)
            def _():
                wait_pre(k + 2, (2, 3))
                post(k + 2, 0, False)
                post(k + 2, 1, False)

        wait_f(k, 3)
        wait_b(k, 3)
        compute(k, 3)
        if final:
            begin(direct_copy(1), valid(3))
        post(ahead, 3, False, ins=not final)
        post(ahead, 4, True, ins=not final)
        if final:
            post(ahead, 3, True, ins=False)

    wait_pre(0, range(4))
    for s in range(2):
        post(0, s, True, outs=False)
        post(0, s, False, outs=False)
    for s in (2, 3):
        post(0, s, False, outs=False)
    start_pre(2)
    for k in range(2, periods):
        send_2(k)
    wait_pre(1, (2, 3))
    post(1, 0, False)
    post(1, 1, False)
    for copy, offset in zip(stat_copies, stat_offsets):
        arrived(copy, valid(-offset))

    def drain(k):
        for i in range(2):
            sent(pre_copy(i, k), either([valid(4), at_head]))
            sent(pre_copy(2 + i, k), either([valid(-4), at_third]))
        for s in range(4):
            sent(fwd_copy(k, s), sends_f())
            sent(back_copy(k, s), sends_b(s))

        @pl.when(k > 0)
        def _():
            sent(back_copy(k, 4), sends_b(4))
            for i in range(2):
                sent(far_copy(k, i), valid((-4, 4)[i]))
                sent(end_far(k, i), (at_last, at_first)[i])

    def finish_far(k):
        for i in range(2):
            wait_far(k + 1, i)
        finish(k)

    def step(k, carry):
        period(k, False)

        @pl.when(k > 0)
        def _():
            start_far(k, 0)

        @pl.when(k > 1)
        def _():
            drain(k - 2)

        @pl.when(k > 2)
        def _():
            finish_far(k - 3)

        return carry

    lax.fori_loop(0, periods - 1, step, 0)
    end = periods - 1
    period(end, True)
    start_far(end, 0)
    finish_far(end - 3)
    forward_back(end)
    finish_far(end - 2)
    for k in range(end - 2, end):
        drain(k)
    for i, copy in enumerate(count_copies):
        sent(copy, valid(-1 - i))
    for copy, offset in zip(stat_copies, stat_offsets):
        sent(copy, valid(offset))
    finish_far(end - 1)
    drain(end)
    for s in (2, 3):
        wait_f(periods, s)
    for s in (0, 1, 3, 4):
        wait_b(periods, s, True)
    for i in range(2):
        arrived(direct_copy(i), (me < blocks - 3, me >= 3)[i])
    finish(end)
    for s in (2, 3):
        sent(fwd_copy(periods, s), sends_f())
    for s in (0, 1, 3, 4):
        sent(back_copy(periods, s), sends_b(s))
    for i in range(2):
        sent(direct_copy(i), valid((-3, 3)[i]))


def keep(a, b, c, a_out, b_out, c_out, sems):
    copies = [
        pltpu.make_async_copy(src, dst, sems.at[i])
        for i, (src, dst) in enumerate(((a, a_out), (b, b_out), (c, c_out)))
    ]
    for copy in copies:
        copy.start()
    for copy in copies:
        copy.wait()


def shards(blocks, q, k, v, g, lse, delta, counts):
    heads = lse.shape[0]
    periods = heads // 4
    rows, width = q.shape
    hbm = pl.BlockSpec(memory_space=pl.ANY)
    vmem = pl.BlockSpec(memory_space=pltpu.VMEM)
    grad = jax.ShapeDtypeStruct((rows, width), jnp.bfloat16)
    dma = pltpu.SemaphoreType.DMA

    def tiles(*lead, dtype=jnp.bfloat16):
        return pltpu.VMEM((*lead, BLK, DIM), dtype)

    grads = pl.pallas_call(
        functools.partial(kernel, blocks, heads),
        out_shape=(grad, grad, grad),
        in_specs=[hbm] * 6 + [pl.BlockSpec(memory_space=pltpu.SMEM)],
        out_specs=(vmem, vmem, vmem),
        scratch_shapes=[
            pltpu.VMEM((rows, width), jnp.bfloat16),
            pltpu.VMEM((rows, width), jnp.bfloat16),
            pltpu.VMEM((rows, width), jnp.bfloat16),
            pltpu.VMEM((rows, width), jnp.bfloat16),
            pltpu.VMEM((periods, 2, BLK, 2 * DIM), jnp.bfloat16),
            pltpu.VMEM((periods, 2, BLK, 2 * DIM), jnp.bfloat16),
            pltpu.VMEM((4, 2 * heads, BLK), jnp.float32),
            pltpu.VMEM((4, 8, BLK), jnp.float32),
            tiles(periods + 1, FWD, 2),
            tiles(periods + 1, BACK, 2),
            tiles(periods + 1, FWD, 2),
            tiles(periods + 1, BACK, 2),
            tiles(periods + 1, 2, 2),
            tiles(periods + 1, 2),
            tiles(periods, 4, 3, dtype=jnp.float32),
            tiles(periods, 4, 3),
            dma((10,)),
            dma((4,)),
            dma((4,)),
            dma((4,)),
            dma((4,)),
            dma((4, periods)),
            dma((4, periods)),
            dma((periods + 1, FWD)),
            dma((periods + 1, FWD)),
            dma((periods + 1, BACK)),
            dma((periods + 1, BACK)),
            dma((periods + 1, 2)),
            dma((periods + 1, 2)),
        ],
        compiler_params=pltpu.CompilerParams(
            collective_id=0, has_side_effects=True, vmem_limit_bytes=123 << 19
        ),
        cost_estimate=pl.CostEstimate(
            flops=40 * heads * BLK * BLK * DIM,
            bytes_accessed=14 * rows * width,
            transcendentals=4 * heads * BLK * BLK,
        ),
    )(q, k, v, g, lse, delta, counts)
    return pl.pallas_call(
        keep,
        out_shape=(grad, grad, grad),
        in_specs=[vmem] * 3,
        out_specs=(hbm, hbm, hbm),
        scratch_shapes=[pltpu.SemaphoreType.DMA((3,))],
        cost_estimate=pl.CostEstimate(
            flops=0, bytes_accessed=6 * rows * width, transcendentals=0
        ),
    )(*grads)


def solution(mesh):
    blocks = mesh.shape["seq"] * mesh.shape["pair"]
    rows = P(("seq", "pair"), None)
    cols = P(None, ("seq", "pair"))
    return jax.shard_map(
        functools.partial(shards, blocks),
        mesh=mesh,
        in_specs=(rows, rows, rows, rows, cols, cols, P(("seq", "pair"))),
        out_specs=(rows, rows, rows),
        check_vma=False,
    )
```

```python
import functools
import math

import jax
import jax.numpy as jnp
from jax import lax
from jax.experimental import pallas as pl
from jax.experimental.pallas import tpu as pltpu
from jax.sharding import PartitionSpec as P

MESH = pl.DeviceIdType.MESH
BLK = 128
DIM = 128
RING = 4
LOG2E = math.log2(math.e)
NEVER = 1e30
NN = (((1,), (0,)), ((), ()))
NT = (((1,), (1,)), ((), ()))
TN = (((0,), (0,)), ((), ()))
FWD, BACK = 4, 5


def dot(a, b, dims=NN):
    return lax.dot_general(a, b, dims, preferred_element_type=jnp.float32)


def either(flags):
    total = flags[0]
    for flag in flags[1:]:
        total = jnp.logical_or(total, flag)
    return total


def both(a, b):
    return jnp.logical_and(a, b)


def kernel(
    blocks,
    heads,
    q_hbm,
    k_hbm,
    v_hbm,
    g_hbm,
    lse_hbm,
    delta_hbm,
    cnt_ref,
    dq_hbm,
    dk_hbm,
    dv_hbm,
    dq_ref,
    dk_ref,
    dv_ref,
    out_sem,
    q_own,
    k_own,
    v_own,
    g_own,
    kv_far,
    qg_far,
    stats,
    counts,
    send_f,
    send_b,
    got_f,
    got_b,
    far_f,
    far_b,
    acc,
    part,
    fetch_sem,
    count_send,
    count_recv,
    stat_send,
    stat_recv,
    pre_send,
    pre_recv,
    f_send,
    f_recv,
    b_send,
    b_recv,
    far_send,
    far_recv,
):
    periods = heads // 4
    x = lax.axis_index("pair")
    me = lax.axis_index("seq") * RING + x
    scale = DIM ** (-0.5)

    def at(offset):
        there = lax.rem(me + (offset + blocks), blocks)
        return (lax.div(there, RING), lax.rem(there, RING))

    def remote(src, dst, send, recv, offset):
        return pltpu.make_async_remote_copy(
            src_ref=src,
            dst_ref=dst,
            send_sem=send,
            recv_sem=recv,
            device_id=at(offset),
            device_id_type=MESH,
        )

    fetches = [
        pltpu.make_async_copy(lse_hbm, stats.at[0, pl.ds(0, heads)], fetch_sem.at[0]),
        pltpu.make_async_copy(delta_hbm, stats.at[0, pl.ds(heads, heads)], fetch_sem.at[1]),
    ]
    operands = ((q_hbm, q_own), (g_hbm, g_own), (k_hbm, k_own), (v_hbm, v_own))
    for n, columns in enumerate((pl.ds(0, 4 * DIM), pl.ds(4 * DIM, (heads - 4) * DIM))):
        fetches += [
            pltpu.make_async_copy(
                hbm.at[:, columns], own.at[:, columns], fetch_sem.at[2 + 4 * n + i]
            )
            for i, (hbm, own) in enumerate(operands)
        ]
    for fetch in fetches:
        fetch.start()
    counts[0] = jnp.full((8, BLK), cnt_ref[0], jnp.int32).astype(jnp.float32)
    counts[1:] = jnp.ones((3, 8, BLK), jnp.float32)

    def valid(offset):
        return me < blocks - offset if offset > 0 else me >= -offset

    def begin(copy, condition):
        pl.when(condition)(copy.start)

    def arrived(copy, condition):
        pl.when(condition)(copy.wait_recv)

    def sent(copy, condition):
        pl.when(condition)(copy.wait_send)

    at_first, at_third = me == 0, me == 3
    at_last, at_head, ahead_of_head = (me == blocks - i for i in (1, 4, 5))

    @pl.when(at_last)
    def _():
        stats[1] = jnp.zeros(stats.shape[1:], stats.dtype)

    barrier = pltpu.get_barrier_semaphore()
    for offset in (-1, 1, 2, 3, -3, -4, 4):

        @pl.when(valid(offset))
        def _(offset=offset):
            pl.semaphore_signal(barrier, 1, device_id=at(offset), device_id_type=MESH)

    near = {3: (0,), 4: (1, blocks - 1), 5: (2, blocks - 2, blocks - 3), 6: (3, blocks - 4)}
    for amount, places in near.items():

        @pl.when(either([me == place for place in places]))
        def _(amount=amount):
            pl.semaphore_wait(barrier, amount)

    @pl.when(both(me > 3, me < blocks - 4))
    def _():
        pl.semaphore_wait(barrier, 7)

    def cols(k, i):
        return pl.ds(pl.multiple_of((4 * k + i) * DIM, DIM), DIM)

    def wide(k, first):
        return pl.ds(pl.multiple_of((4 * k + first) * DIM, 2 * DIM), 2 * DIM)

    def pre_copy(i, k, early=False):
        own = ((k_hbm, v_hbm, q_hbm, g_hbm) if early else (k_own, v_own, q_own, g_own))[i]
        src = own.at[:, wide(k, 0 if i < 2 else 2)]
        dst = (kv_far if i < 2 else qg_far).at[k, i % 2]
        return remote(src, dst, pre_send.at[i, k], pre_recv.at[i, k], 4 if i < 2 else -4)

    def end_copies(i, k, early):
        own = ((k_hbm, v_hbm, q_hbm, g_hbm) if early else (k_own, v_own, q_own, g_own))[i]
        got, recv = (got_b, b_recv) if i < 2 else (got_f, f_recv)
        return [
            remote(
                own.at[:, cols(k, s if i < 2 else 2 + s)],
                got.at[k, s, i % 2],
                pre_send.at[i, k],
                recv.at[k, s],
                3 if i < 2 else -3,
            )
            for s in range(2)
        ]

    def start_pre(k, early=False):
        for i in range(4):
            begin(pre_copy(i, k, early), valid(4 if i < 2 else -4))
            for copy in end_copies(i, k, early):
                begin(copy, at_head if i < 2 else at_third)

    start_pre(0, True)

    count_copies = [
        remote(counts.at[0], counts.at[i], count_send.at[i], count_recv.at[i], -i)
        for i in (1, 2, 3)
    ]
    for i, copy in enumerate(count_copies):
        begin(copy, valid(-1 - i))

    stat_copies = [
        remote(stats.at[0], stats.at[i], stat_send.at[i], stat_recv.at[i], offset)
        for i, offset in ((1, -1), (2, 1), (3, -3))
    ]
    for fetch in fetches[:2]:
        fetch.wait()
    stat_offsets = (-1, 1, -3)
    for copy, offset in zip(stat_copies, stat_offsets):
        begin(copy, valid(offset))
    for fetch in fetches[2:6]:
        fetch.wait()
    place = cnt_ref[0]
    p0, p1, p2, p3 = (place == i for i in (1, 2, 3, 4))

    def content(kind, i, k, side):
        if kind == "kv":
            return (k_own, v_own)[side][:, cols(k, i)]
        if kind == "qg":
            return (q_own, g_own)[side][:, cols(k, i)]
        if kind == "kvx":
            return kv_far[k, side, :, i * DIM : (i + 1) * DIM]
        if kind == "qgx":
            return qg_far[k, side, :, (i - 2) * DIM : (i - 1) * DIM]
        if kind == "dkv":
            return part[k - 1, i, 1 + side]
        return part[k - 1, i + side, 0]

    def fwd_copy(k, s):
        return remote(send_f.at[k, s], got_f.at[k, s], f_send.at[k, s], f_recv.at[k, s], 1)

    def back_copy(k, s):
        return remote(send_b.at[k, s], got_b.at[k, s], b_send.at[k, s], b_recv.at[k, s], -1)

    def far_copy(k, i):
        if i == 0:
            src, dst = got_f.at[k, pl.ds(2, 2)], far_f.at[k]
        else:
            src, dst = got_b.at[k, 4], far_b.at[k]
        return remote(src, dst, far_send.at[k, i], far_recv.at[k, i], -4 if i == 0 else 4)

    def direct_copy(i):
        if i == 0:
            src, dst = part.at[periods - 1, pl.ds(0, 2), pl.ds(1, 2)], far_f.at[periods]
        else:
            src, dst = part.at[periods - 1, pl.ds(2, 2), 0], far_b.at[periods]
        at_end = (far_send.at[periods, i], far_recv.at[periods, i])
        return remote(src, dst, *at_end, -3 if i == 0 else 3)

    def end_far(k, i):
        if i == 0:
            src, dst = part.at[k - 1, pl.ds(0, 2), pl.ds(1, 2)], far_f.at[k]
        else:
            src, dst = part.at[k - 1, pl.ds(2, 2), 0], far_b.at[k]
        send_sem = (f_send if i == 0 else b_send).at[k, 0]
        return remote(src, dst, send_sem, far_recv.at[k, i], -3 if i == 0 else 3)

    def sends_f():
        return me < blocks - 1

    def sends_b(s):
        return both(me > 0, me != blocks - 4) if s in (2, 3) else me > 0

    def wait_f(k, s):
        arrived(fwd_copy(k, s), me > 0) if s in (2, 3) else fwd_copy(k, s).wait_recv()

    def wait_b(k, s, flush=False):
        if s in (2, 3):
            arrived(back_copy(k, s), both(me < blocks - 1, me != blocks - 5))
        elif s == 4 or flush:
            arrived(back_copy(k, s), me < blocks - 1)
        else:
            back_copy(k, s).wait_recv()

    def start_far(k, i):
        begin(far_copy(k, i), valid((-4, 4)[i]))
        begin(end_far(k, i), (at_last, at_first)[i])

    def wait_far(k, i):
        arrived(far_copy(k, i), (me < blocks - 3, me >= 3)[i])

    def send(table, k, s, back, ins=True, outs=True):
        stage = send_b if back else send_f
        table = [e for e in table if (ins and e[1][0] != "d") or (outs and e[1][0] == "d")]
        for side in range(2):
            value = content(table[-1][1], table[-1][2], k, side)
            for flag, kind, i in table[:-1]:
                value = jnp.where(flag, content(kind, i, k, side), value)
            stage[k, s, side] = value
        begin((back_copy if back else fwd_copy)(k, s), sends_b(s) if back else sends_f())

    def wait_pre(k, which):
        for i in which:
            arrived(pre_copy(i, k), valid(-4 if i < 2 else 4))

    def send_2(k):
        send(((p1, "kv", 3), (None, "qg", 2)), k, 2, True)

    send_2(0)
    send(((None, "qg", 3),), 0, 3, True)
    for fetch in fetches[6:]:
        fetch.wait()
    send_2(1)
    start_pre(1)
    for i, copy in enumerate(count_copies):
        arrived(copy, valid(1 + i))
    c1, c2, c3 = (jnp.max(counts[i]) for i in (1, 2, 3))
    p0l4 = both(p0, c3 == 4.0)
    p1l4 = both(p1, c2 == 4.0)
    p2l4 = both(p2, c1 == 4.0)
    p0s = both(both(p0, c1 == 2.0), c3 != 4.0)
    p1s = both(p1, c2 != 4.0)
    p1g3 = both(p1, c1 == 3.0)
    p1l3 = both(p1g3, c2 != 4.0)
    p2l3 = both(p2, c1 != 4.0)
    last = c1 == 1.0

    fwd_table = (
        ((p0l4, "kv", 2), (either([p0s, p1l4]), "kv", 0), (p2l4, "qg", 0), (last, "qgx", 2)),
        ((p0l4, "kv", 3), (either([p0s, p1l4]), "kv", 1), (p2l4, "qg", 1), (last, "qgx", 3)),
        (
            (either([p0s, p1l4]), "kv", 2),
            (either([p0l4, p1l3, p2l4]), "dq", 0),
            (p3, "dkv", 0),
        ),
        (
            (p0s, "kv", 3),
            (p0l4, "dkv", 3),
            (either([p1g3, p2l4]), "dq", 2),
            (p3, "dkv", 1),
        ),
    )
    back_table = (
        ((p0, "kvx", 0), (either([p2l4, p1s]), "dkv", 0), (None, "qg", 0)),
        ((p0, "kvx", 1), (either([p2l4, p1s]), "dkv", 1), (None, "qg", 1)),
        ((p1, "kv", 3), (None, "qg", 2)),
        ((p1, "dkv", 2), (None, "qg", 3)),
        ((p1, "dkv", 3), (p2l4, "dkv", 2), (p3, "dq", 0), (None, "dq", 2)),
    )

    def post(k, s, back, ins=True, outs=True):
        send((back_table if back else fwd_table)[s], k, s, back, ins, outs)

    row = lax.broadcasted_iota(jnp.int32, (BLK, BLK), 0)
    col = lax.broadcasted_iota(jnp.int32, (BLK, BLK), 1)
    causal = col >= row

    has_k = (either([p3, p2l4, p1s]),) * 2 + (either([p1, p2l4]), either([p0l4, p1]))
    has_q = (either([p0l4, p2l4, p3, p1l3]),) * 2 + (either([p0l4, p1g3, p2l4]),) * 2
    own_q_far_k = (has_k[0], has_k[1], p1, p1)
    far_q_own_k = (both(has_q[0], jnp.logical_not(p3)),) * 2 + (has_q[2], has_q[3])

    def compute(k, i):
        f = [got_f.at[k, s] for s in range(FWD)]
        b = [got_b.at[k, s] for s in range(BACK)]

        def far_kv(side):
            if i < 2:
                value = jnp.where(p3, b[i][side], f[i][side])
            elif i == 2:
                value = jnp.where(p1l4, f[0][side], f[2][side])
            else:
                value = jnp.where(p1l4, f[1][side], f[3][side])
                value = jnp.where(p0, b[2][side], value)
            return jnp.where(has_k[i], value, jnp.zeros_like(value))

        def far_qg(side):
            if i < 2:
                value = jnp.where(p3, f[i][side], b[i][side])
            else:
                value = jnp.where(p0, f[i - 2][side], b[i][side])
            return jnp.where(has_q[i], value, jnp.zeros_like(value))

        here = cols(k, i)
        keys = jnp.concatenate([k_own[:, here], far_kv(0)], axis=0)
        values = jnp.concatenate([v_own[:, here], far_kv(1)], axis=0)
        queries = jnp.concatenate([q_own[:, here], far_qg(0)], axis=0)
        grads = jnp.concatenate([g_own[:, here], far_qg(1)], axis=0)
        h = 4 * k + i
        lse_row, delta_row = pl.ds(h, 1), pl.ds(heads + h, 1)

        def far_row(at_row):
            if i < 2:
                return jnp.where(p3, stats[2, at_row, :], stats[1, at_row, :])
            return jnp.where(p0, stats[3, at_row, :], stats[1, at_row, :])

        lse = [stats[0, lse_row, :] * LOG2E, far_row(lse_row) * LOG2E]
        delta = [stats[0, delta_row, :], far_row(delta_row)]
        scores = dot(keys, queries, NT)
        dprobs = dot(values, grads, NT)
        halves, dscores = [], []
        for u in range(2):
            for t in range(2):
                shift = lse[t]
                if u or t:
                    allowed = (
                        both(has_k[i], has_q[i])
                        if u and t
                        else (own_q_far_k[i] if u else far_q_own_k[i])
                    )
                    shift = jnp.where(allowed, shift, jnp.full_like(shift, NEVER))
                tile = (slice(u * BLK, (u + 1) * BLK), slice(t * BLK, (t + 1) * BLK))
                prob = jnp.exp2(scores[tile] * (scale * LOG2E) - shift)
                if not (u or t):
                    prob = jnp.where(causal, prob, 0.0)
                halves.append(prob.astype(jnp.bfloat16))
                dscores.append((prob * (dprobs[tile] - delta[t]) * scale).astype(jnp.bfloat16))

        def square(tiles):
            return jnp.concatenate(
                [jnp.concatenate(tiles[:2], axis=1), jnp.concatenate(tiles[2:], axis=1)], axis=0
            )

        half, dscore = square(halves), square(dscores)
        for n, value in enumerate(
            (dot(dscore, keys, TN), dot(dscore, queries), dot(half, grads))
        ):
            acc[k, i, n] = value[:BLK]
            part[k, i, n] = value[BLK:].astype(jnp.bfloat16)

    def out_copies(k):
        columns = pl.ds(pl.multiple_of(4 * k * DIM, 4 * DIM), 4 * DIM)
        return [
            pltpu.make_async_copy(ref.at[:, columns], hbm.at[:, columns], out_sem.at[n, k])
            for n, (ref, hbm) in enumerate(
                ((dq_ref, dq_hbm), (dk_ref, dk_hbm), (dv_ref, dv_hbm))
            )
        ]

    def finish(k):
        f = [got_f.at[k + 1, s] for s in range(FWD)]
        b = [got_b.at[k + 1, s] for s in range(BACK)]
        back_f, back_b = far_f.at[k + 1], far_b.at[k + 1]

        def add(total, flag, value):
            value = value.astype(jnp.float32)
            return total + jnp.where(flag, value, jnp.zeros_like(value))

        p1l4_p2_p3 = either([p1l4, p2, p3])
        p2_p3 = either([p2, p3])
        p0g2_p1l4 = either([p0l4, p0s, p1l4])
        for i in range(4):
            here = cols(k, i)
            if i < 2:
                value = jnp.where(p2l4, b[4][i], f[2][i])
                total = add(acc[k, i, 0], p1l4_p2_p3, value)
            else:
                total = add(acc[k, i, 0], p2_p3, f[3][i - 2])
                total = add(total, p3, back_b[i - 2])
            dq_ref[:, here] = total.astype(jnp.bfloat16)
            for side, out in enumerate((dk_ref, dv_ref)):
                if i < 2:
                    value = jnp.where(p0l4, back_f[i, side], b[i][side])
                elif i == 2:
                    value = jnp.where(p1l4, b[4][side], b[3][side])
                else:
                    value = jnp.where(p1l4, f[3][side], b[4][side])
                out[:, here] = add(acc[k, i, 1 + side], p0g2_p1l4, value).astype(jnp.bfloat16)
        for copy in out_copies(k):
            copy.start()

    def forward_back(k):
        wait_b(k, 4)
        start_far(k, 1)

    def period(k, final):
        ahead = k + 1
        if not final:

            @pl.when(k < periods - 3)
            def _():
                start_pre(k + 3)

        wait_f(k, 0)
        wait_b(k, 0)
        compute(k, 0)
        if not final:
            wait_pre(ahead, (0, 1))
        post(ahead, 0, True, ins=not final)
        wait_f(k, 1)
        wait_b(k, 1)
        compute(k, 1)
        post(ahead, 1, True, ins=not final)
        post(ahead, 2, False, ins=not final)
        if final:
            begin(direct_copy(0), valid(-3))

        @pl.when(k > 1)
        def _():
            forward_back(k - 1)

        wait_f(k, 2)
        wait_b(k, 2)
        compute(k, 2)
        if not final:
            post(ahead, 3, True)

            @pl.when(k < periods - 2)
            def _():
                wait_pre(k + 2, (2, 3))
                post(k + 2, 0, False)
                post(k + 2, 1, False)

        wait_f(k, 3)
        wait_b(k, 3)
        compute(k, 3)
        if final:
            begin(direct_copy(1), valid(3))
        post(ahead, 3, False, ins=not final)
        post(ahead, 4, True, ins=not final)
        if final:
            post(ahead, 3, True, ins=False)

    wait_pre(0, range(4))
    for s in range(2):
        post(0, s, True, outs=False)
        post(0, s, False, outs=False)
    for s in (2, 3):
        post(0, s, False, outs=False)
    start_pre(2)
    for k in range(2, periods):
        send_2(k)
    wait_pre(1, (2, 3))
    post(1, 0, False)
    post(1, 1, False)
    for copy, offset in zip(stat_copies, stat_offsets):
        arrived(copy, valid(-offset))

    def drain(k):
        for i in range(2):
            sent(pre_copy(i, k), either([valid(4), at_head]))
            sent(pre_copy(2 + i, k), either([valid(-4), at_third]))
        for s in range(4):
            sent(fwd_copy(k, s), sends_f())
            sent(back_copy(k, s), sends_b(s))

        @pl.when(k > 0)
        def _():
            sent(back_copy(k, 4), sends_b(4))
            for i in range(2):
                sent(far_copy(k, i), valid((-4, 4)[i]))
                sent(end_far(k, i), (at_last, at_first)[i])

    def finish_far(k):
        for i in range(2):
            wait_far(k + 1, i)
        finish(k)

    def step(k, carry):
        period(k, False)

        @pl.when(k > 0)
        def _():
            start_far(k, 0)

        @pl.when(k > 1)
        def _():
            drain(k - 2)

        @pl.when(k > 2)
        def _():
            finish_far(k - 3)

        return carry

    lax.fori_loop(0, periods - 1, step, 0)
    end = periods - 1
    period(end, True)
    start_far(end, 0)
    finish_far(end - 3)
    forward_back(end)
    finish_far(end - 2)
    for k in range(end - 2, end):
        drain(k)
    for i, copy in enumerate(count_copies):
        sent(copy, valid(-1 - i))
    for copy, offset in zip(stat_copies, stat_offsets):
        sent(copy, valid(offset))
    finish_far(end - 1)
    drain(end)
    for s in (2, 3):
        wait_f(periods, s)
    for s in (0, 1, 3, 4):
        wait_b(periods, s, True)
    for i in range(2):
        arrived(direct_copy(i), (me < blocks - 3, me >= 3)[i])
    finish(end)
    for s in (2, 3):
        sent(fwd_copy(periods, s), sends_f())
    for s in (0, 1, 3, 4):
        sent(back_copy(periods, s), sends_b(s))
    for i in range(2):
        sent(direct_copy(i), valid((-3, 3)[i]))
    for k in range(periods):
        for copy in out_copies(k):
            copy.wait()


def keep(a, b, c, a_out, b_out, c_out, held, in_sem, out_sem):
    pairs = []
    for half in range(2):
        rows = pl.ds(half * (BLK // 2), BLK // 2)
        for i, (src, dst) in enumerate(((a, a_out), (b, b_out), (c, c_out))):
            pairs.append(
                (
                    pltpu.make_async_copy(src.at[rows], held.at[i, rows], in_sem.at[half, i]),
                    pltpu.make_async_copy(held.at[i, rows], dst.at[rows], out_sem.at[half, i]),
                )
            )
    for fetch, _ in pairs:
        fetch.start()
    for fetch, write in pairs:
        fetch.wait()
        write.start()
    for _, write in pairs:
        write.wait()


def shards(blocks, q, k, v, g, lse, delta, counts):
    heads = lse.shape[0]
    periods = heads // 4
    rows, width = q.shape
    hbm = pl.BlockSpec(memory_space=pl.ANY)
    grad = jax.ShapeDtypeStruct((rows, width), jnp.bfloat16)
    dma = pltpu.SemaphoreType.DMA

    def tiles(*lead, dtype=jnp.bfloat16):
        return pltpu.VMEM((*lead, BLK, DIM), dtype)

    grads = pl.pallas_call(
        functools.partial(kernel, blocks, heads),
        out_shape=(grad, grad, grad),
        in_specs=[hbm] * 6 + [pl.BlockSpec(memory_space=pltpu.SMEM)],
        out_specs=(hbm, hbm, hbm),
        scratch_shapes=[
            pltpu.VMEM((rows, width), jnp.bfloat16),
            pltpu.VMEM((rows, width), jnp.bfloat16),
            pltpu.VMEM((rows, width), jnp.bfloat16),
            dma((3, periods)),
            pltpu.VMEM((rows, width), jnp.bfloat16),
            pltpu.VMEM((rows, width), jnp.bfloat16),
            pltpu.VMEM((rows, width), jnp.bfloat16),
            pltpu.VMEM((rows, width), jnp.bfloat16),
            pltpu.VMEM((periods, 2, BLK, 2 * DIM), jnp.bfloat16),
            pltpu.VMEM((periods, 2, BLK, 2 * DIM), jnp.bfloat16),
            pltpu.VMEM((4, 2 * heads, BLK), jnp.float32),
            pltpu.VMEM((4, 8, BLK), jnp.float32),
            tiles(periods + 1, FWD, 2),
            tiles(periods + 1, BACK, 2),
            tiles(periods + 1, FWD, 2),
            tiles(periods + 1, BACK, 2),
            tiles(periods + 1, 2, 2),
            tiles(periods + 1, 2),
            tiles(periods, 4, 3, dtype=jnp.float32),
            tiles(periods, 4, 3),
            dma((10,)),
            dma((4,)),
            dma((4,)),
            dma((4,)),
            dma((4,)),
            dma((4, periods)),
            dma((4, periods)),
            dma((periods + 1, FWD)),
            dma((periods + 1, FWD)),
            dma((periods + 1, BACK)),
            dma((periods + 1, BACK)),
            dma((periods + 1, 2)),
            dma((periods + 1, 2)),
        ],
        compiler_params=pltpu.CompilerParams(
            collective_id=0, has_side_effects=True, vmem_limit_bytes=123 << 19
        ),
        cost_estimate=pl.CostEstimate(
            flops=40 * heads * BLK * BLK * DIM,
            bytes_accessed=14 * rows * width,
            transcendentals=4 * heads * BLK * BLK,
        ),
    )(q, k, v, g, lse, delta, counts)
    return pl.pallas_call(
        keep,
        out_shape=(grad, grad, grad),
        in_specs=[hbm] * 3,
        out_specs=(hbm, hbm, hbm),
        scratch_shapes=[pltpu.VMEM((3, rows, width), jnp.bfloat16), dma((2, 3)), dma((2, 3))],
        compiler_params=pltpu.CompilerParams(vmem_limit_bytes=123 << 19),
        cost_estimate=pl.CostEstimate(
            flops=0, bytes_accessed=6 * rows * width, transcendentals=0
        ),
    )(*grads)


def solution(mesh):
    blocks = mesh.shape["seq"] * mesh.shape["pair"]
    rows = P(("seq", "pair"), None)
    cols = P(None, ("seq", "pair"))
    return jax.shard_map(
        functools.partial(shards, blocks),
        mesh=mesh,
        in_specs=(rows, rows, rows, rows, cols, cols, P(("seq", "pair"))),
        out_specs=(rows, rows, rows),
        check_vma=False,
    )
```
